32 devices in a mesh: row: 4 (over x, core), col: 8 (over z, y).
Axes of the slice: x: 2, y: 2, z: 4, core: 2. Of those that a mesh axis runs over, the one named last changes fastest.
Arguments:
- stiffness: float32 [2048, 2048], P('row', 'col'), may hold values from -0.6 to 4.5
Outputs:
- factored: float32 [2048, 2048], P('row', 'col')
The draws below stay inside these ranges and needn't reach their ends.
All inputs are finite; a program needn't handle non-finite values.
Results may differ from the reference program's by a relative error of at most 0.0001.
Values sent between devices are 32-bit elements; how exact they have to be, the bound alone decides.
No kernel may reach another device: no remote copies, remote signals or barrier semaphores. Data moves between devices by JAX's collectives and lax.ppermute only.
A program may use at most 64 MiB of HBM per device.

```python
import jax
import jax.numpy as jnp
from jax import lax

SNODE_W = 256
SNODES = 4
ORDER = 2048


def draw_stiffness(key, part):
    key = jax.random.fold_in(key, 7)
    key_rough, key_link, key_diag = jax.random.split(key, 3)
    rough = jax.random.uniform(key_rough, (ORDER, ORDER), jnp.float32, -1.0, 1.0)
    linked = jax.random.uniform(key_link, (ORDER, ORDER), jnp.float32, -1.0, 1.0)
    reach = 0.05
    window = SNODES * SNODE_W
    rough = (rough + rough.T) * (0.15 / jnp.sqrt(jnp.float32(ORDER)))
    places = jnp.arange(ORDER, dtype=jnp.int32)
    inside = places < window
    coupling = jnp.where(inside[:, None] & jnp.logical_not(inside[None, :]), linked, jnp.zeros_like(linked))
    link_scale = 5.37 / (jnp.sqrt(jnp.float32(window)) + jnp.sqrt(jnp.float32(ORDER - window)))
    coupling = (coupling + coupling.T) * link_scale
    spots = places.astype(jnp.float32)
    smooth = reach * jnp.exp(-jnp.abs(spots[:, None] - spots[None, :]) / 64.0)
    diag_part = 3.7 + 0.6 * jax.random.uniform(key_diag, (ORDER,), jnp.float32)
    return rough + coupling + smooth + jnp.diag(diag_part)


def setup_inputs(seed: int = 0) -> dict:
    seeds = jax.random.split(jax.random.key(seed), 2)
    return {
        "stiffness": draw_stiffness(jax.random.fold_in(seeds[1], 71), 0),
    }


def reference(stiffness):
    working = stiffness
    for section in range(SNODES):
        first_col = section * SNODE_W
        end_col = first_col + SNODE_W
        factor = jnp.linalg.cholesky(working[first_col:end_col, first_col:end_col])
        panel = jax.scipy.linalg.solve_triangular(factor, working[first_col:, first_col:end_col].T, lower=True).T
        working = working.at[first_col:, first_col:end_col].set(panel)
        low_panel = panel[SNODE_W:]
        update = lax.dot_general(low_panel, low_panel, (((1,), (1,)), ((), ())), precision=lax.Precision.HIGHEST)
        working = working.at[end_col:, end_col:].add(-update)
    row_ids = jnp.arange(ORDER, dtype=jnp.int32)[:, None]
    col_ids = jnp.arange(ORDER, dtype=jnp.int32)[None, :]
    window = SNODES * SNODE_W
    keep = jnp.where(col_ids < window, row_ids >= col_ids, row_ids >= window)
    return jnp.where(keep, working, jnp.zeros_like(working))
```

```python
import functools

import jax
import jax.numpy as jnp
from jax import lax
from jax.experimental import pallas as pl
from jax.experimental.pallas import tpu as pltpu
from jax.sharding import PartitionSpec as P

SNODES = 4
LANES = 128
SUB = 8
f32 = jnp.float32
bf16 = jnp.bfloat16
VMEM = pl.BlockSpec(memory_space=pltpu.VMEM)
SMEM = pl.BlockSpec(memory_space=pltpu.SMEM)
PARAMS = pltpu.CompilerParams(vmem_limit_bytes=56 * 2**20)


def lane_copy(tile, lane):
    return jnp.broadcast_to(tile[:, lane : lane + 1], (SUB, LANES))


def row_copy(tile, row):
    return jnp.broadcast_to(tile[row : row + 1, :], (SUB, LANES))


def factor_half(block):
    lane = lax.broadcasted_iota(jnp.int32, (SUB, LANES), 1)
    sub = lax.broadcasted_iota(jnp.int32, (SUB, LANES), 0)
    n = LANES // SUB
    tiles = [block[SUB * t : SUB * t + SUB, :] for t in range(n)]
    upper, inverse = [], []
    diag = [lane_copy(tiles[0], k) for k in range(SUB)]
    for p in range(n):
        rows, base = tiles[p], SUB * p
        up = jnp.zeros((SUB, LANES), f32)
        inv = up
        pivot_rows, scales, roots = [], [], []
        for j in range(SUB):
            at = base + j
            root = lax.rsqrt(row_copy(diag[j], j))
            column = diag[j] * root
            up_row = row_copy(rows, j) * root
            inv_row = jnp.where(lane == at, root, up_row)
            rows = jnp.where(lane == at, 0.0, rows) - column * inv_row
            scale = [None] * SUB
            for k in range(j + 1, SUB):
                scale[k] = row_copy(column, k)
                diag[k] = diag[k] - column * scale[k]
            up = jnp.where(sub == j, up_row, up)
            inv = jnp.where(sub == j, inv_row, inv)
            pivot_rows.append(jnp.where((lane > at) & (lane < base + SUB), 0.0, inv_row))
            scales.append(scale)
            roots.append(root)
        upper.append(up)
        inverse.append(inv)
        ahead = None
        for t in range(p + 1, n):
            left = [lane_copy(tiles[t], base + k) for k in range(SUB)]
            if t == p + 1:
                ahead = [lane_copy(tiles[t], base + SUB + k) for k in range(SUB)]
            rest = jnp.where((lane >= base) & (lane < base + SUB), 0.0, tiles[t])
            for j in range(SUB):
                column = left[j] * roots[j]
                rest = rest - column * pivot_rows[j]
                for k in range(j + 1, SUB):
                    left[k] = left[k] - column * scales[j][k]
                if t == p + 1:
                    for k in range(SUB):
                        ahead[k] = ahead[k] - column * row_copy(column, k)
            tiles[t] = rest
        diag = ahead
    return jnp.concatenate(upper, 0), jnp.concatenate(inverse, 0)


def split(x):
    high = x.astype(bf16)
    return high, (x - high.astype(f32)).astype(bf16)


def as_left(x):
    high, low = split(x)
    return jnp.concatenate([high, high, low], axis=1)


def as_right(x):
    high, low = split(x)
    return jnp.concatenate([high, low, high], axis=1)


def dot_t(left, right):
    return lax.dot_general(left, right, (((1,), (1,)), ((), ())), preferred_element_type=f32)


def dot_plain(a, b):
    def dot(x, y):
        return lax.dot_general(x, y, (((1,), (0,)), ((), ())), preferred_element_type=f32)

    (ah, al), (bh, bl) = split(a), split(b)
    return dot(ah, bh) + dot(ah, bl) + dot(al, bh)


def lower(x):
    row = lax.broadcasted_iota(jnp.int32, x.shape, 0)
    col = lax.broadcasted_iota(jnp.int32, x.shape, 1)
    return jnp.where(row >= col, x, 0.0)


def factor_block(block, factor_ref, inv_ref, col):
    h = LANES
    up_a, inv_a = factor_half(block[:h, :h])
    inv_a = lower(inv_a)
    low = dot_t(as_left(block[h:, :h]), as_right(inv_a))
    up_b, inv_b = factor_half(block[h:, h:] - dot_t(as_left(low), as_right(low)))
    inv_b = lower(inv_b)
    inv_low = -dot_plain(inv_b, dot_plain(low, inv_a))
    zero = jnp.zeros((h, h), f32)
    factor_ref[:h, col : col + h] = lower(up_a.T)
    factor_ref[:h, col + h : col + 2 * h] = zero
    factor_ref[h:, col : col + h] = low
    factor_ref[h:, col + h : col + 2 * h] = lower(up_b.T)
    inv = jnp.concatenate([jnp.concatenate([inv_a, zero], 1), jnp.concatenate([inv_low, inv_b], 1)], 0)
    inv_ref[...] = as_right(inv)


def chain_body(take, k, width, refs):
    inv_refs, right_refs = refs[:k], refs[k : 2 * k]
    factor_ref, inv_ref, right_ref, left = refs[2 * k :]
    w = width
    for j in range(k):
        rest = take(j)
        if j > 0:
            rest = rest - dot_t(left[:, : 3 * w * j], right_refs[j][:, : 3 * w * j])
        row = dot_t(as_left(rest), inv_refs[j][...])
        factor_ref[:, w * j : w * j + w] = row
        left[:, 3 * w * j : 3 * w * (j + 1)] = as_left(row)
        right_ref[:, 3 * w * j : 3 * w * (j + 1)] = as_right(row)
    block = take(k)
    if k > 0:
        block = block - dot_t(left[:, : 3 * w * k], right_ref[:, : 3 * w * k])
    else:
        right_ref[...] = jnp.zeros_like(right_ref)
    factor_block(block, factor_ref, inv_ref, w * k)


def chain_call(kernel, k, width, inputs, specs, state):
    invs, rights = state
    wide = 3 * width * max(1, k)
    factor, inv, right = pl.pallas_call(
        kernel,
        out_shape=[
            jax.ShapeDtypeStruct((width, (k + 1) * width), f32),
            jax.ShapeDtypeStruct((width, 3 * width), bf16),
            jax.ShapeDtypeStruct((width, wide), bf16),
        ],
        in_specs=specs + [VMEM] * (2 * k),
        out_specs=[VMEM] * 3,
        scratch_shapes=[pltpu.VMEM((width, wide), bf16)],
        compiler_params=PARAMS,
        name=f"chain{k}",
    )(*inputs, *invs, *rights)
    return factor, (invs + [inv], rights + [right])


def solve_rows(take, rows, extra, inv_refs, right_refs, left, right, factor_rows, width):
    w = width
    for k in range(SNODES):
        rest = take(k)
        if k > 0:
            rest = rest - dot_t(left[:, : 3 * w * k], right_refs[k][:, : 3 * w * k])
        row = dot_t(as_left(rest), inv_refs[k][...])
        left[:, 3 * w * k : 3 * w * (k + 1)] = as_left(row)
        right[:, 3 * w * k : 3 * w * (k + 1)] = as_right(row[rows:])
        factor_rows(k, row[:rows])


def write_tile(pos_ref, take, tile_ref, inv_refs, right_refs, factor_refs, out_ref, left, right, width):
    row_index, col_index = pos_ref[0], pos_ref[1]
    rows = out_ref.shape[0]
    blocks = rows // width
    inside = SNODES * width // rows
    top = row_index < inside

    @pl.when(jnp.logical_not(top))
    def _():
        def factor_rows(k, value):
            @pl.when(col_index == k)
            def _():
                out_ref[...] = value

        solve_rows(take, rows, width, inv_refs, right_refs, left, right, factor_rows, width)

        @pl.when(col_index >= SNODES)
        def _():
            out_ref[...] = tile_ref[...] - dot_t(left[:rows], right[...])

    @pl.when(top)
    def _():
        out_ref[...] = jnp.zeros_like(out_ref)
        for i in range(SNODES):
            for j in range(i + 1):

                @pl.when((row_index == i // blocks) & (col_index == j))
                def _():
                    at = (i % blocks) * width
                    out_ref[at : at + width, :] = factor_refs[i][:, j * width : (j + 1) * width]


def plain_chain(k, width, *refs):
    block_ref = refs[0]
    chain_body(lambda j: block_ref[:, j * width : (j + 1) * width], k, width, refs[1:])


def plain_tile(width, *refs):
    pos_ref, below_ref, tile_ref = refs[:3]
    n = SNODES
    inv_refs, right_refs, factor_refs = refs[3 : 3 + n], refs[3 + n : 3 + 2 * n], refs[3 + 2 * n : 3 + 3 * n]
    out_ref, left, right = refs[3 + 3 * n :]
    write_tile(
        pos_ref,
        lambda k: below_ref[:, k * width : (k + 1) * width],
        tile_ref, inv_refs, right_refs, factor_refs, out_ref, left, right, width,
    )


def tile_call(kernel, inputs, state, factors, rows, width):
    invs, rights = state
    wide = 3 * width * SNODES
    return pl.pallas_call(
        kernel,
        out_shape=jax.ShapeDtypeStruct((rows, width), f32),
        in_specs=[SMEM] + [VMEM] * (len(inputs) - 1 + 3 * SNODES),
        out_specs=VMEM,
        scratch_shapes=[pltpu.VMEM((rows + width, wide), bf16), pltpu.VMEM((width, wide), bf16)],
        compiler_params=PARAMS,
        name="tile",
    )(*inputs, *invs, *rights, *factors)


def any_mesh(stiffness):
    rows, width = stiffness.shape
    row_index, col_index = lax.axis_index("row"), lax.axis_index("col")
    inside = SNODES * width // rows
    zero = jnp.zeros_like(stiffness)
    own_rows = lax.psum(
        jnp.concatenate([jnp.where(col_index == j, stiffness, zero) for j in range(SNODES)], 1), "col"
    )
    window = lax.psum(
        jnp.concatenate([jnp.where(row_index == i, own_rows, jnp.zeros_like(own_rows)) for i in range(inside)], 0), "row"
    )
    own_cols = lax.psum(jnp.concatenate([jnp.where(row_index == i, stiffness, zero) for i in range(inside)], 0), "row")
    state, factors = ([], []), []
    for k in range(SNODES):
        block = window[k * width : (k + 1) * width, : (k + 1) * width]
        factor, state = chain_call(functools.partial(plain_chain, k, width), k, width, [block], [VMEM], state)
        factors.append(factor)
    below = jnp.concatenate([own_rows, own_cols.T], 0)
    pos = jnp.stack([row_index, col_index]).astype(jnp.int32)
    return tile_call(
        functools.partial(plain_tile, width), [pos, below, stiffness], state, factors, rows, width
    )


def chain_first(width, pos_ref, a_ref, b_ref, *refs):
    even = (pos_ref[0] % 2) == 0
    chain_body(lambda j: jnp.where(even, a_ref[...], b_ref[...]), 0, width, refs)


def chain_second(width, pos_ref, a_ref, b_ref, *refs):
    even = (pos_ref[0] % 2) == 0
    chain_body(lambda j: jnp.where(even, a_ref[j], b_ref[j]), 1, width, refs)


def chain_later(k, width, pos_ref, a_ref, b_ref, a_other, b_other, *refs):
    core = pos_ref[0] % 2
    first = (pos_ref[1] % 2) == k % 2

    def take(j):
        own = core == j // 2
        mine = jnp.where(own, a_ref[j % 2], a_other[j % 2])
        other = jnp.where(own, b_ref[j % 2], b_other[j % 2])
        return jnp.where(first, mine, other)

    chain_body(take, k, width, refs)


def box_tile(width, *refs):
    pos_ref, tile_ref = refs[:2]
    below, crossed, other = refs[2:6], refs[6:10], refs[10:14]
    rest = refs[14:]
    n = SNODES
    inv_refs, right_refs, factor_refs = rest[:n], rest[n : 2 * n], rest[2 * n : 3 * n]
    out_ref, left, right, work = rest[3 * n :]
    row_index, col_index = pos_ref[0], pos_ref[1]
    core = row_index % 2
    w = width

    @pl.when((row_index >= 2) & (col_index < n))
    def _():
        for m in range(4):
            for k in range(n):

                @pl.when((col_index ^ m) == k)
                def _():
                    work[k, :w, :] = below[m][0]
                    work[k, w : 2 * w, :] = below[m][1]

    @pl.when((row_index >= 2) & (col_index >= n))
    def _():
        for k in range(n):
            for place in range(3):
                want = col_index if place == 2 else n + 2 * core + place
                for m in range(4):

                    @pl.when((col_index ^ m) == want)
                    def _():
                        work[k, place * w : (place + 1) * w, :] = jnp.where(
                            core == k // 2, crossed[m][k % 2], other[m][k % 2]
                        )

    write_tile(
        pos_ref, lambda k: work[k], tile_ref, inv_refs, right_refs, factor_refs, out_ref, left, right, width
    )


def swap(x, pair):
    perm = []
    for r in range(4):
        for c in range(8):
            pr, pc = pair(r, c)
            perm.append((r * 8 + c, pr * 8 + pc))
    return lax.ppermute(x, ("row", "col"), perm)


def across(members):
    def pair(r, c):
        if r < 2 and c < 4 and members(r, c):
            return r + 2, c + 4
        if r >= 2 and c >= 4 and members(r - 2, c - 4):
            return r - 2, c - 4
        return r, c

    return pair


def core_pair(r, c):
    return r ^ 1, c


def x_pair(r, c):
    return r ^ 2, c


def y_pair(r, c):
    return r, c ^ 1


def z_pair(r, c):
    return r, c ^ 2


def mixed(r, c):
    return (r >= 2) != (c >= 4)


def some(pair, members):
    return lambda r, c: pair(r, c) if members(r, c) else (r, c)


def box_mesh(stiffness):
    rows, width = stiffness.shape
    r, c = lax.axis_index("row"), lax.axis_index("col")
    pos = jnp.stack([r, c]).astype(jnp.int32)
    blocks = stiffness.reshape(2, width, width)
    first = (r == 0) & (c == 0)

    d = blocks[0]
    d = jnp.where((r == 2) & (c == 4), swap(d, across(lambda r, c: (r, c) == (0, 0))), d)
    q = jnp.where(r < 2, blocks.transpose(0, 2, 1), blocks)
    d = jnp.where(c % 2 == 0, d, swap(d, y_pair))
    d = jnp.where((c // 2) % 2 == 0, d, swap(d, z_pair))
    d = jnp.where((r >= 2) & (c < 4), swap(d, x_pair), d)
    d_other = swap(d, core_pair)

    xq = swap(q, x_pair)
    e = swap(q, across(lambda r, c: (r, c) == (0, 1)))
    e = jnp.where(r < 2, q, jnp.where(c < 4, xq, e))
    e = jnp.where(c % 2 == 1, e, swap(e, y_pair))
    e = jnp.where((c // 2) % 2 == 0, e, swap(e, z_pair))
    e_other = swap(e, core_pair)

    g = swap(q, across(lambda r, c: c >= 2))
    g = jnp.where(r < 2, q, jnp.where(c < 4, xq, g))
    gy = swap(g, y_pair)
    odd = (c // 2) % 2 == 1
    g = jnp.where(odd, g, swap(g, z_pair))
    gy = jnp.where(odd, gy, swap(gy, z_pair))
    g_other, gy_other = swap(g, core_pair), swap(gy, core_pair)

    yq, zq = swap(q, some(y_pair, mixed)), swap(q, some(z_pair, mixed))
    yzq = swap(zq, some(y_pair, mixed))
    xzq, xyq = swap(zq, x_pair), swap(yq, x_pair)
    xyzq = swap(xzq, y_pair)
    crossed = [xq, xyq, xzq, xyzq]
    other = [swap(v, core_pair) for v in crossed]

    state, factors = ([], []), []
    for k in range(SNODES):
        if k == 0:
            kernel, inputs = chain_first, [pos, d, d_other]
        elif k == 1:
            kernel, inputs = chain_second, [pos, e, e_other]
        else:
            kernel, inputs = functools.partial(chain_later, k), [pos, g, gy, g_other, gy_other]
        factor, state = chain_call(
            functools.partial(kernel, width), k, width, inputs, [SMEM] + [VMEM] * (len(inputs) - 1), state
        )
        factors.append(factor)
    invs, rights = state
    wide = 3 * width * SNODES
    inputs = [pos, stiffness, q, yq, zq, yzq, *crossed, *other]
    return pl.pallas_call(
        functools.partial(box_tile, width),
        out_shape=jax.ShapeDtypeStruct((rows, width), f32),
        in_specs=[SMEM] + [VMEM] * (len(inputs) - 1 + 3 * SNODES),
        out_specs=VMEM,
        scratch_shapes=[
            pltpu.VMEM((rows + width, wide), bf16),
            pltpu.VMEM((width, wide), bf16),
            pltpu.VMEM((SNODES, rows + width, width), f32),
        ],
        compiler_params=PARAMS,
        name="tile",
    )(*inputs, *invs, *rights, *factors)


def solution(mesh):
    box = (mesh.shape["row"], mesh.shape["col"]) == (4, 8)

    def on_device(stiffness):
        rows, width = stiffness.shape
        return box_mesh(stiffness) if box and rows == 2 * width else any_mesh(stiffness)

    return jax.shard_map(
        on_device, mesh=mesh, in_specs=(P("row", "col"),), out_specs=P("row", "col"), check_vma=False
    )
```

```python
import functools

import jax
import jax.numpy as jnp
from jax import lax
from jax.experimental import pallas as pl
from jax.experimental.pallas import tpu as pltpu
from jax.sharding import PartitionSpec as P

SNODES = 4
LANES = 128
SUB = 8
f32 = jnp.float32
bf16 = jnp.bfloat16
VMEM = pl.BlockSpec(memory_space=pltpu.VMEM)
SMEM = pl.BlockSpec(memory_space=pltpu.SMEM)
PARAMS = pltpu.CompilerParams(vmem_limit_bytes=16 * 2**20)
TILE_PARAMS = pltpu.CompilerParams(vmem_limit_bytes=36 * 2**20)
COST = pl.CostEstimate(flops=1000, bytes_accessed=1024, transcendentals=0)


def lane_copy(tile, lane):
    return jnp.broadcast_to(tile[:, lane : lane + 1], (SUB, LANES))


def row_copy(tile, row):
    return jnp.broadcast_to(tile[row : row + 1, :], (SUB, LANES))


def factor_half(block):
    lane = lax.broadcasted_iota(jnp.int32, (SUB, LANES), 1)
    sub = lax.broadcasted_iota(jnp.int32, (SUB, LANES), 0)
    n = LANES // SUB
    tiles = [block[SUB * t : SUB * t + SUB, :] for t in range(n)]
    upper, inverse = [], []
    diag = [lane_copy(tiles[0], k) for k in range(SUB)]
    for p in range(n):
        rows, base = tiles[p], SUB * p
        up = jnp.zeros((SUB, LANES), f32)
        inv = up
        pivot_rows, scales, roots = [], [], []
        for j in range(SUB):
            at = base + j
            root = lax.rsqrt(row_copy(diag[j], j))
            column = diag[j] * root
            up_row = row_copy(rows, j) * root
            inv_row = jnp.where(lane == at, root, up_row)
            rows = jnp.where(lane == at, 0.0, rows) - column * inv_row
            scale = [None] * SUB
            for k in range(j + 1, SUB):
                scale[k] = row_copy(column, k)
                diag[k] = diag[k] - column * scale[k]
            up = jnp.where(sub == j, up_row, up)
            inv = jnp.where(sub == j, inv_row, inv)
            pivot_rows.append(jnp.where((lane > at) & (lane < base + SUB), 0.0, inv_row))
            scales.append(scale)
            roots.append(root)
        upper.append(up)
        inverse.append(inv)
        ahead = None
        for t in range(p + 1, n):
            left = [lane_copy(tiles[t], base + k) for k in range(SUB)]
            if t == p + 1:
                ahead = [lane_copy(tiles[t], base + SUB + k) for k in range(SUB)]
            rest = jnp.where((lane >= base) & (lane < base + SUB), 0.0, tiles[t])
            for j in range(SUB):
                column = left[j] * roots[j]
                rest = rest - column * pivot_rows[j]
                for k in range(j + 1, SUB):
                    left[k] = left[k] - column * scales[j][k]
                if t == p + 1:
                    for k in range(SUB):
                        ahead[k] = ahead[k] - column * row_copy(column, k)
            tiles[t] = rest
        diag = ahead
    return jnp.concatenate(upper, 0), jnp.concatenate(inverse, 0)


def split(x):
    high = x.astype(bf16)
    return high, (x - high.astype(f32)).astype(bf16)


def as_left(x):
    high, low = split(x)
    return jnp.concatenate([high, high, low], axis=1)


def as_right(x):
    high, low = split(x)
    return jnp.concatenate([high, low, high], axis=1)


def dot_t(left, right):
    return lax.dot_general(left, right, (((1,), (1,)), ((), ())), preferred_element_type=f32)


def dot_plain(a, b):
    def dot(x, y):
        return lax.dot_general(x, y, (((1,), (0,)), ((), ())), preferred_element_type=f32)

    (ah, al), (bh, bl) = split(a), split(b)
    return dot(ah, bh) + dot(ah, bl) + dot(al, bh)


def lower(x):
    row = lax.broadcasted_iota(jnp.int32, x.shape, 0)
    col = lax.broadcasted_iota(jnp.int32, x.shape, 1)
    return jnp.where(row >= col, x, 0.0)


def factor_block(block, factor_ref, col):
    h = LANES
    up_a, inv_a = factor_half(block[:h, :h])
    inv_a = lower(inv_a)
    low = dot_t(as_left(block[h:, :h]), as_right(inv_a))
    up_b, inv_b = factor_half(block[h:, h:] - dot_t(as_left(low), as_right(low)))
    inv_b = lower(inv_b)
    inv_low = -dot_plain(inv_b, dot_plain(low, inv_a))
    zero = jnp.zeros((h, h), f32)
    factor_ref[:h, col : col + h] = lower(up_a.T)
    factor_ref[:h, col + h : col + 2 * h] = zero
    factor_ref[h:, col : col + h] = low
    factor_ref[h:, col + h : col + 2 * h] = lower(up_b.T)
    return jnp.concatenate([jnp.concatenate([inv_a, zero], 1), jnp.concatenate([inv_low, inv_b], 1)], 0)


def chain_body(take, k, width, refs):
    inv_refs, right_refs = refs[:k], refs[k : 2 * k]
    factor_ref, inv_ref, right_ref, left = refs[2 * k :]
    w = width
    for j in range(k):
        rest = take(j)
        if j > 0:
            rest = rest - dot_t(left[:, : 3 * w * j], right_refs[j][:, : 3 * w * j])
        row = dot_t(as_left(rest), inv_refs[j][...])
        factor_ref[:, w * j : w * j + w] = row
        left[:, 3 * w * j : 3 * w * (j + 1)] = as_left(row)
        right_ref[:, 3 * w * j : 3 * w * (j + 1)] = as_right(row)
    block = take(k)
    if k > 0:
        block = block - dot_t(left[:, : 3 * w * k], right_ref[:, : 3 * w * k])
    else:
        right_ref[...] = jnp.zeros_like(right_ref)
    inv_ref[...] = as_right(factor_block(block, factor_ref, w * k))


def chain_call(kernel, k, width, inputs, specs, state):
    invs, rights = state
    wide = 3 * width * max(1, k)
    factor, inv, right = pl.pallas_call(
        kernel,
        out_shape=[
            jax.ShapeDtypeStruct((width, (k + 1) * width), f32),
            jax.ShapeDtypeStruct((width, 3 * width), bf16),
            jax.ShapeDtypeStruct((width, wide), bf16),
        ],
        in_specs=specs + [VMEM] * (2 * k),
        out_specs=[VMEM] * 3,
        scratch_shapes=[pltpu.VMEM((width, wide), bf16)],
        compiler_params=PARAMS,
        cost_estimate=COST,
        name=f"chain{k}",
    )(*inputs, *invs, *rights)
    return factor, (invs + [inv], rights + [right])


def solve_rows(take, rows, extra, inv_refs, right_refs, left, right, factor_rows, width):
    w = width
    for k in range(SNODES):
        rest = take(k)
        if k > 0:
            rest = rest - dot_t(left[:, : 3 * w * k], right_refs[k][:, : 3 * w * k])
        row = dot_t(as_left(rest), inv_refs[k][...])
        left[:, 3 * w * k : 3 * w * (k + 1)] = as_left(row)
        right[:, 3 * w * k : 3 * w * (k + 1)] = as_right(row[rows:])
        factor_rows(k, row[:rows])


def write_tile(pos_ref, take, tile_ref, inv_refs, right_refs, factor_refs, out_ref, left, right, width):
    row_index, col_index = pos_ref[0], pos_ref[1]
    rows = out_ref.shape[0]
    blocks = rows // width
    inside = SNODES * width // rows
    top = row_index < inside

    @pl.when(jnp.logical_not(top))
    def _():
        def factor_rows(k, value):
            @pl.when(col_index == k)
            def _():
                out_ref[...] = value

        solve_rows(take, rows, width, inv_refs, right_refs, left, right, factor_rows, width)

        @pl.when(col_index >= SNODES)
        def _():
            out_ref[...] = tile_ref[...] - dot_t(left[:rows], right[...])

    @pl.when(top)
    def _():
        out_ref[...] = jnp.zeros_like(out_ref)
        for i in range(SNODES):
            for j in range(i + 1):

                @pl.when((row_index == i // blocks) & (col_index == j))
                def _():
                    at = (i % blocks) * width
                    out_ref[at : at + width, :] = factor_refs[i][:, j * width : (j + 1) * width]


def plain_chain(k, width, *refs):
    block_ref = refs[0]
    chain_body(lambda j: block_ref[:, j * width : (j + 1) * width], k, width, refs[1:])


def plain_tile(width, *refs):
    pos_ref, below_ref, tile_ref = refs[:3]
    n = SNODES
    inv_refs, right_refs, factor_refs = refs[3 : 3 + n], refs[3 + n : 3 + 2 * n], refs[3 + 2 * n : 3 + 3 * n]
    out_ref, left, right = refs[3 + 3 * n :]
    write_tile(
        pos_ref,
        lambda k: below_ref[:, k * width : (k + 1) * width],
        tile_ref, inv_refs, right_refs, factor_refs, out_ref, left, right, width,
    )


def tile_call(kernel, inputs, state, factors, rows, width):
    invs, rights = state
    wide = 3 * width * SNODES
    return pl.pallas_call(
        kernel,
        out_shape=jax.ShapeDtypeStruct((rows, width), f32),
        in_specs=[SMEM] + [VMEM] * (len(inputs) - 1 + 3 * SNODES),
        out_specs=VMEM,
        scratch_shapes=[pltpu.VMEM((rows + width, wide), bf16), pltpu.VMEM((width, wide), bf16)],
        compiler_params=TILE_PARAMS,
        cost_estimate=COST,
        name="tile",
    )(*inputs, *invs, *rights, *factors)


def any_mesh(stiffness):
    rows, width = stiffness.shape
    row_index, col_index = lax.axis_index("row"), lax.axis_index("col")
    inside = SNODES * width // rows
    zero = jnp.zeros_like(stiffness)
    own_rows = lax.psum(
        jnp.concatenate([jnp.where(col_index == j, stiffness, zero) for j in range(SNODES)], 1), "col"
    )
    window = lax.psum(
        jnp.concatenate([jnp.where(row_index == i, own_rows, jnp.zeros_like(own_rows)) for i in range(inside)], 0), "row"
    )
    own_cols = lax.psum(jnp.concatenate([jnp.where(row_index == i, stiffness, zero) for i in range(inside)], 0), "row")
    state, factors = ([], []), []
    for k in range(SNODES):
        block = window[k * width : (k + 1) * width, : (k + 1) * width]
        factor, state = chain_call(functools.partial(plain_chain, k, width), k, width, [block], [VMEM], state)
        factors.append(factor)
    below = jnp.concatenate([own_rows, own_cols.T], 0)
    pos = jnp.stack([row_index, col_index]).astype(jnp.int32)
    return tile_call(
        functools.partial(plain_tile, width), [pos, below, stiffness], state, factors, rows, width
    )


def chain_early(k, width, pos_ref, a_ref, b_ref, *refs):
    even = (pos_ref[0] % 2) == 0
    chain_body(lambda j: jnp.where(even, a_ref[k + j], b_ref[k + j]), k, width, refs)


def chain_later(k, width, pos_ref, a_ref, b_ref, *refs):
    core = pos_ref[0] % 2
    chain_body(lambda j: jnp.where(core == j // 2, a_ref[j % 2], b_ref[j % 2]), k, width, refs)


def box_tile(width, *refs):
    pos_ref, tile_ref = refs[:2]
    below, crossed, other = refs[2:6], refs[6], refs[7]
    rest = refs[8:]
    n = SNODES
    inv_refs, right_refs, factor_refs = rest[:n], rest[n : 2 * n], rest[2 * n : 3 * n]
    out_ref, left, right, work = rest[3 * n :]
    row_index, col_index = pos_ref[0], pos_ref[1]
    core = row_index % 2
    w = width

    @pl.when((row_index >= 2) & (col_index < n))
    def _():
        for m in range(4):
            k = col_index ^ m
            work[k, :w, :] = below[m][0]
            work[k, w : 2 * w, :] = below[m][1]

    @pl.when((row_index >= 2) & (col_index >= n))
    def _():
        for m in range(4):
            column = (col_index ^ m) - n

            def place(at):
                for k in range(n):
                    work[k, at * w : (at + 1) * w, :] = jnp.where(core == k // 2, crossed[m, k % 2], other[m, k % 2])

            if m == 0:
                place(2)
            for at in range(2):
                pl.when(column == 2 * core + at)(functools.partial(place, at))

    write_tile(
        pos_ref, lambda k: work[k], tile_ref, inv_refs, right_refs, factor_refs, out_ref, left, right, width
    )


def swap(x, pair):
    perm = []
    for r in range(4):
        for c in range(8):
            pr, pc = pair(r, c)
            if (pr, pc) != (r, c):
                perm.append((r * 8 + c, pr * 8 + pc))
    return lax.ppermute(x, ("row", "col"), perm)


def core_pair(r, c):
    return r ^ 1, c


def x_pair(r, c):
    return r ^ 2, c


def y_pair(r, c):
    return r, c ^ 1


def z_pair(r, c):
    return r, c ^ 2


def after(x, *others):
    return lax.optimization_barrier((x, *others))[0]


def some(pair, members):
    return lambda r, c: pair(r, c) if members(r, c) else (r, c)


def chosen(pairs):
    table = {a: b for p, q in pairs for a, b in ((p, q), (q, p))}
    return lambda r, c: table.get((r, c), (r, c))


def box_mesh(stiffness):
    rows, width = stiffness.shape
    r, c = lax.axis_index("row"), lax.axis_index("col")
    pos = jnp.stack([r, c]).astype(jnp.int32)
    blocks = stiffness.reshape(2, width, width)
    even, near = c % 2 == 0, (c // 2) % 2 == 0
    schur, corner = (r >= 2) & (c >= 4), (r < 2) & (c >= 4)
    q = jnp.where(r < 2, blocks.transpose(0, 2, 1), blocks)

    beside = [((r, c), (r, c + 1)) for r in (0, 1) for c in (4, 6)]
    below = [((r, c), (r, c + 1)) for r in (2, 3) for c in (0, 2)]
    hop = swap(q, chosen([((0, 0), (2, 4)), ((0, 1), (2, 5))] + beside))
    hop_far = swap(q, chosen([((0, 0), (2, 6)), ((0, 1), (2, 7))] + below))
    zq = swap(q, lambda r, c: z_pair(r, c) if (r < 2 or c < 4) and not (r == 1 and c < 2) else (r, c))
    xq = swap(q, x_pair)
    hop_late = swap(xq, chosen([((r, c), (r, c + 4)) for r in (2, 3) for c in (2, 3)]))
    hop_later = swap(xq, chosen([((r, c), (r, c + 2)) for r in (2, 3) for c in (2, 3)]))
    xz = swap(zq, x_pair)
    to_schur = some(x_pair, lambda r, c: c >= 4)
    xy = swap(hop, to_schur)

    def held(on_near, on_far):
        return jnp.where(near, on_near, on_far)

    m = held(
        jnp.where(schur, hop, jnp.where(r < 2, q, xq)),
        jnp.where(schur, hop_far, zq),
    )
    m = after(jnp.where(corner, zq, m), hop_late)
    ym = swap(m, some(y_pair, lambda r, c: (r < 2 and c >= 4) or r == 0 or (r == 2 and c not in (2, 3))))
    n = jnp.concatenate([jnp.where(even, m[:1], ym[:1]), jnp.where(even, ym, m)], 0)
    late = chosen([((0, c), (2, c)) for c in (2, 3)])
    n = jnp.where((r == 2) & (c < 4) & jnp.logical_not(near), swap(n, late), n)
    n = after(n, hop_later, xz)
    n_other = swap(n, core_pair)

    state, factors = ([], []), []
    factor, state = chain_call(
        functools.partial(chain_early, 0, width), 0, width, [pos, n, n_other], [SMEM, VMEM, VMEM], state
    )
    factors.append(factor)

    cross = swap(
        jnp.where(corner, ym, zq),
        lambda r, c: x_pair(r, c) if c >= 4 else y_pair(r, c) if r >= 2 else (r, c),
    )
    g_near = after(hop_later, factor)
    g = held(
        jnp.where(schur, g_near, jnp.where(r < 2, zq, xz)),
        jnp.where(schur, hop_late, jnp.where(r < 2, q, xq)),
    )
    yg = swap(g, some(y_pair, lambda r, c: r >= 2 or c < 4))
    factor, state = chain_call(
        functools.partial(chain_early, 1, width), 1, width, [pos, after(n, g), n_other], [SMEM, VMEM, VMEM], state
    )
    factors.append(factor)
    yg = after(yg, factor)
    g2, g3 = jnp.where(even, g, yg), jnp.where(even, yg, g)
    g2_other, g3_other = swap(g2, core_pair), swap(g3, core_pair)
    g2 = after(g2, xy, g3_other)
    factor, state = chain_call(
        functools.partial(chain_later, 2, width), 2, width, [pos, g2, g2_other], [SMEM, VMEM, VMEM], state
    )
    factors.append(factor)
    crossed = jnp.stack([xq, xy, xz, after(cross, factor)])
    other = swap(crossed, some(core_pair, lambda r, c: r >= 2 and c >= 4))
    factor, state = chain_call(
        functools.partial(chain_later, 3, width), 3, width, [pos, g3, g3_other], [SMEM, VMEM, VMEM], state
    )
    factors.append(factor)
    invs, rights = state
    wide = 3 * width * SNODES
    inputs = [pos, stiffness, blocks, hop_far, zq, cross, crossed, other]
    return pl.pallas_call(
        functools.partial(box_tile, width),
        out_shape=jax.ShapeDtypeStruct((rows, width), f32),
        in_specs=[SMEM] + [VMEM] * (len(inputs) - 1 + 3 * SNODES),
        out_specs=VMEM,
        scratch_shapes=[
            pltpu.VMEM((rows + width, wide), bf16),
            pltpu.VMEM((width, wide), bf16),
            pltpu.VMEM((SNODES, rows + width, width), f32),
        ],
        compiler_params=TILE_PARAMS,
        cost_estimate=COST,
        name="tile",
    )(*inputs, *invs, *rights, *factors)


def solution(mesh):
    box = (mesh.shape["row"], mesh.shape["col"]) == (4, 8)

    def on_device(stiffness):
        rows, width = stiffness.shape
        return box_mesh(stiffness) if box and rows == 2 * width else any_mesh(stiffness)

    return jax.shard_map(
        on_device, mesh=mesh, in_specs=(P("row", "col"),), out_specs=P("row", "col"), check_vma=False
    )
```

```python
import functools

import jax
import jax.numpy as jnp
from jax import lax
from jax.experimental import pallas as pl
from jax.experimental.pallas import tpu as pltpu
from jax.sharding import PartitionSpec as P

SNODES = 4
LANES = 128
SUB = 8
f32 = jnp.float32
bf16 = jnp.bfloat16
VMEM = pl.BlockSpec(memory_space=pltpu.VMEM)
SMEM = pl.BlockSpec(memory_space=pltpu.SMEM)
PARAMS = pltpu.CompilerParams(vmem_limit_bytes=16 * 2**20)
TILE_PARAMS = pltpu.CompilerParams(vmem_limit_bytes=36 * 2**20)
COST = pl.CostEstimate(flops=1000, bytes_accessed=1024, transcendentals=0)


def lane_copy(tile, lane):
    return jnp.broadcast_to(tile[:, lane : lane + 1], (SUB, LANES))


def row_copy(tile, row):
    return jnp.broadcast_to(tile[row : row + 1, :], (SUB, LANES))


def factor_half(block):
    lane = lax.broadcasted_iota(jnp.int32, (SUB, LANES), 1)
    sub = lax.broadcasted_iota(jnp.int32, (SUB, LANES), 0)
    n = LANES // SUB
    tiles = [block[SUB * t : SUB * t + SUB, :] for t in range(n)]
    upper, inverse = [], []
    diag = [lane_copy(tiles[0], k) for k in range(SUB)]
    for p in range(n):
        rows, base = tiles[p], SUB * p
        up = jnp.zeros((SUB, LANES), f32)
        inv = up
        pivot_rows, scales, roots = [], [], []
        for j in range(SUB):
            at = base + j
            root = lax.rsqrt(row_copy(diag[j], j))
            column = diag[j] * root
            up_row = row_copy(rows, j) * root
            inv_row = jnp.where(lane == at, root, up_row)
            rows = jnp.where(lane == at, 0.0, rows) - column * inv_row
            scale = [None] * SUB
            for k in range(j + 1, SUB):
                scale[k] = row_copy(column, k)
                diag[k] = diag[k] - column * scale[k]
            up = jnp.where(sub == j, up_row, up)
            inv = jnp.where(sub == j, inv_row, inv)
            pivot_rows.append(jnp.where((lane > at) & (lane < base + SUB), 0.0, inv_row))
            scales.append(scale)
            roots.append(root)
        upper.append(up)
        inverse.append(inv)
        ahead = None
        for t in range(p + 1, n):
            left = [lane_copy(tiles[t], base + k) for k in range(SUB)]
            if t == p + 1:
                ahead = [lane_copy(tiles[t], base + SUB + k) for k in range(SUB)]
            rest = jnp.where((lane >= base) & (lane < base + SUB), 0.0, tiles[t])
            for j in range(SUB):
                column = left[j] * roots[j]
                rest = rest - column * pivot_rows[j]
                for k in range(j + 1, SUB):
                    left[k] = left[k] - column * scales[j][k]
                if t == p + 1:
                    for k in range(SUB):
                        ahead[k] = ahead[k] - column * row_copy(column, k)
            tiles[t] = rest
        diag = ahead
    return jnp.concatenate(upper, 0), jnp.concatenate(inverse, 0)


def split(x):
    high = x.astype(bf16)
    return high, (x - high.astype(f32)).astype(bf16)


def as_left(x):
    high, low = split(x)
    return jnp.concatenate([high, high, low], axis=1)


def as_right(x):
    high, low = split(x)
    return jnp.concatenate([high, low, high], axis=1)


def dot_t(left, right):
    return lax.dot_general(left, right, (((1,), (1,)), ((), ())), preferred_element_type=f32)


def dot_plain(a, b):
    def dot(x, y):
        return lax.dot_general(x, y, (((1,), (0,)), ((), ())), preferred_element_type=f32)

    (ah, al), (bh, bl) = split(a), split(b)
    return dot(ah, bh) + dot(ah, bl) + dot(al, bh)


def lower(x):
    row = lax.broadcasted_iota(jnp.int32, x.shape, 0)
    col = lax.broadcasted_iota(jnp.int32, x.shape, 1)
    return jnp.where(row >= col, x, 0.0)


def factor_block(block, factor_ref, col):
    h = LANES
    up_a, inv_a = factor_half(block[:h, :h])
    inv_a = lower(inv_a)
    low = dot_t(as_left(block[h:, :h]), as_right(inv_a))
    up_b, inv_b = factor_half(block[h:, h:] - dot_t(as_left(low), as_right(low)))
    inv_b = lower(inv_b)
    inv_low = -dot_plain(inv_b, dot_plain(low, inv_a))
    zero = jnp.zeros((h, h), f32)
    factor_ref[:h, col : col + h] = lower(up_a.T)
    factor_ref[:h, col + h : col + 2 * h] = zero
    factor_ref[h:, col : col + h] = low
    factor_ref[h:, col + h : col + 2 * h] = lower(up_b.T)
    return jnp.concatenate([jnp.concatenate([inv_a, zero], 1), jnp.concatenate([inv_low, inv_b], 1)], 0)


def chain_body(take, k, width, refs):
    inv_refs, right_refs = refs[:k], refs[k : 2 * k]
    factor_ref, inv_ref, right_ref, left = refs[2 * k :]
    w = width
    for j in range(k):
        rest = take(j)
        if j > 0:
            rest = rest - dot_t(left[:, : 3 * w * j], right_refs[j][:, : 3 * w * j])
        row = dot_t(as_left(rest), inv_refs[j][...])
        factor_ref[:, w * j : w * j + w] = row
        left[:, 3 * w * j : 3 * w * (j + 1)] = as_left(row)
        right_ref[:, 3 * w * j : 3 * w * (j + 1)] = as_right(row)
    block = take(k)
    if k > 0:
        block = block - dot_t(left[:, : 3 * w * k], right_ref[:, : 3 * w * k])
    else:
        right_ref[...] = jnp.zeros_like(right_ref)
    inv_ref[...] = as_right(factor_block(block, factor_ref, w * k))


def chain_call(kernel, k, width, inputs, specs, state):
    invs, rights = state
    wide = 3 * width * max(1, k)
    factor, inv, right = pl.pallas_call(
        kernel,
        out_shape=[
            jax.ShapeDtypeStruct((width, (k + 1) * width), f32),
            jax.ShapeDtypeStruct((width, 3 * width), bf16),
            jax.ShapeDtypeStruct((width, wide), bf16),
        ],
        in_specs=specs + [VMEM] * (2 * k),
        out_specs=[VMEM] * 3,
        scratch_shapes=[pltpu.VMEM((width, wide), bf16)],
        compiler_params=PARAMS,
        cost_estimate=COST,
        name=f"chain{k}",
    )(*inputs, *invs, *rights)
    return factor, (invs + [inv], rights + [right])


def solve_rows(take, rows, extra, inv_refs, right_refs, left, right, factor_rows, width):
    w = width
    for k in range(SNODES):
        rest = take(k)
        if k > 0:
            rest = rest - dot_t(left[:, : 3 * w * k], right_refs[k][:, : 3 * w * k])
        row = dot_t(as_left(rest), inv_refs[k][...])
        left[:, 3 * w * k : 3 * w * (k + 1)] = as_left(row)
        right[:, 3 * w * k : 3 * w * (k + 1)] = as_right(row[rows:])
        factor_rows(k, row[:rows])


def write_tile(pos_ref, take, tile_ref, inv_refs, right_refs, factor_refs, out_ref, left, right, width):
    row_index, col_index = pos_ref[0], pos_ref[1]
    rows = out_ref.shape[0]
    blocks = rows // width
    inside = SNODES * width // rows
    top = row_index < inside

    @pl.when(jnp.logical_not(top))
    def _():
        def factor_rows(k, value):
            @pl.when(col_index == k)
            def _():
                out_ref[...] = value

        solve_rows(take, rows, width, inv_refs, right_refs, left, right, factor_rows, width)

        @pl.when(col_index >= SNODES)
        def _():
            out_ref[...] = tile_ref[...] - dot_t(left[:rows], right[...])

    @pl.when(top)
    def _():
        out_ref[...] = jnp.zeros_like(out_ref)
        for i in range(SNODES):
            for j in range(i + 1):

                @pl.when((row_index == i // blocks) & (col_index == j))
                def _():
                    at = (i % blocks) * width
                    out_ref[at : at + width, :] = factor_refs[i][:, j * width : (j + 1) * width]


def plain_chain(k, width, *refs):
    block_ref = refs[0]
    chain_body(lambda j: block_ref[:, j * width : (j + 1) * width], k, width, refs[1:])


def plain_tile(width, *refs):
    pos_ref, below_ref, tile_ref = refs[:3]
    n = SNODES
    inv_refs, right_refs, factor_refs = refs[3 : 3 + n], refs[3 + n : 3 + 2 * n], refs[3 + 2 * n : 3 + 3 * n]
    out_ref, left, right = refs[3 + 3 * n :]
    write_tile(
        pos_ref,
        lambda k: below_ref[:, k * width : (k + 1) * width],
        tile_ref, inv_refs, right_refs, factor_refs, out_ref, left, right, width,
    )


def tile_call(kernel, inputs, state, factors, rows, width):
    invs, rights = state
    wide = 3 * width * SNODES
    return pl.pallas_call(
        kernel,
        out_shape=jax.ShapeDtypeStruct((rows, width), f32),
        in_specs=[SMEM] + [VMEM] * (len(inputs) - 1 + 3 * SNODES),
        out_specs=VMEM,
        scratch_shapes=[pltpu.VMEM((rows + width, wide), bf16), pltpu.VMEM((width, wide), bf16)],
        compiler_params=TILE_PARAMS,
        cost_estimate=COST,
        name="tile",
    )(*inputs, *invs, *rights, *factors)


def any_mesh(stiffness):
    rows, width = stiffness.shape
    row_index, col_index = lax.axis_index("row"), lax.axis_index("col")
    inside = SNODES * width // rows
    zero = jnp.zeros_like(stiffness)
    own_rows = lax.psum(
        jnp.concatenate([jnp.where(col_index == j, stiffness, zero) for j in range(SNODES)], 1), "col"
    )
    window = lax.psum(
        jnp.concatenate([jnp.where(row_index == i, own_rows, jnp.zeros_like(own_rows)) for i in range(inside)], 0), "row"
    )
    own_cols = lax.psum(jnp.concatenate([jnp.where(row_index == i, stiffness, zero) for i in range(inside)], 0), "row")
    state, factors = ([], []), []
    for k in range(SNODES):
        block = window[k * width : (k + 1) * width, : (k + 1) * width]
        factor, state = chain_call(functools.partial(plain_chain, k, width), k, width, [block], [VMEM], state)
        factors.append(factor)
    below = jnp.concatenate([own_rows, own_cols.T], 0)
    pos = jnp.stack([row_index, col_index]).astype(jnp.int32)
    return tile_call(
        functools.partial(plain_tile, width), [pos, below, stiffness], state, factors, rows, width
    )


def chain_early(k, width, pos_ref, a_ref, b_ref, *refs):
    even = (pos_ref[0] % 2) == 0
    chain_body(lambda j: jnp.where(even, a_ref[k + j], b_ref[k + j]), k, width, refs)


def chain_later(k, width, pos_ref, a_ref, b_ref, *refs):
    core = pos_ref[0] % 2
    chain_body(lambda j: jnp.where(core == j // 2, a_ref[j % 2], b_ref[j % 2]), k, width, refs)


def box_tile(width, *refs):
    pos_ref, tile_ref = refs[:2]
    below, crossed, other = refs[2:6], refs[6], refs[7]
    rest = refs[8:]
    n = SNODES
    inv_refs, right_refs, factor_refs = rest[:n], rest[n : 2 * n], rest[2 * n : 3 * n]
    out_ref, left, right, work = rest[3 * n :]
    row_index, col_index = pos_ref[0], pos_ref[1]
    core = row_index % 2
    w = width

    @pl.when((row_index >= 2) & (col_index < n))
    def _():
        for m in range(4):
            k = col_index ^ m
            work[k, :w, :] = below[m][0]
            work[k, w : 2 * w, :] = below[m][1]

    @pl.when((row_index >= 2) & (col_index >= n))
    def _():
        for m in range(4):
            column = (col_index ^ m) - n

            def place(at):
                for k in range(n):
                    work[k, at * w : (at + 1) * w, :] = jnp.where(core == k // 2, crossed[m, k % 2], other[m, k % 2])

            if m == 0:
                place(2)
            for at in range(2):
                pl.when(column == 2 * core + at)(functools.partial(place, at))

    write_tile(
        pos_ref, lambda k: work[k], tile_ref, inv_refs, right_refs, factor_refs, out_ref, left, right, width
    )


def swap(x, pair):
    perm = []
    for r in range(4):
        for c in range(8):
            pr, pc = pair(r, c)
            if (pr, pc) != (r, c):
                perm.append((r * 8 + c, pr * 8 + pc))
    return lax.ppermute(x, ("row", "col"), perm)


def core_pair(r, c):
    return r ^ 1, c


def x_pair(r, c):
    return r ^ 2, c


def y_pair(r, c):
    return r, c ^ 1


def z_pair(r, c):
    return r, c ^ 2


def after(x, *others):
    return lax.optimization_barrier((x, *others))[0]


def some(pair, members):
    return lambda r, c: pair(r, c) if members(r, c) else (r, c)


def chosen(pairs):
    table = {a: b for p, q in pairs for a, b in ((p, q), (q, p))}
    return lambda r, c: table.get((r, c), (r, c))


def box_mesh(stiffness):
    rows, width = stiffness.shape
    r, c = lax.axis_index("row"), lax.axis_index("col")
    pos = jnp.stack([r, c]).astype(jnp.int32)
    blocks = stiffness.reshape(2, width, width)
    even, near = c % 2 == 0, (c // 2) % 2 == 0
    schur, corner = (r >= 2) & (c >= 4), (r < 2) & (c >= 4)
    q = jnp.where(r < 2, blocks.transpose(0, 2, 1), blocks)

    beside = [((r, c), (r, c + 1)) for r in (0, 1) for c in (4, 6)]
    below = [((r, c), (r, c + 1)) for r in (2, 3) for c in (0, 2)]
    hop = swap(q, chosen([((0, 0), (2, 4)), ((0, 1), (2, 5))] + beside))
    hop_far = swap(q, chosen([((0, 0), (2, 6)), ((0, 1), (2, 7))] + below))
    zq = swap(q, lambda r, c: z_pair(r, c) if (r < 2 or c < 4) and not (r == 1 and c < 2) else (r, c))
    xq = swap(q, x_pair)
    hop_late = swap(xq, chosen([((r, c), (r, c + 4)) for r in (2, 3) for c in (2, 3)]))
    hop_later = swap(xq, chosen([((r, c), (r, c + 2)) for r in (2, 3) for c in (2, 3)]))
    to_schur = some(x_pair, lambda r, c: c >= 4)
    near_z = swap(zq, some(x_pair, lambda r, c: c < 2))
    xz = swap(zq, to_schur)
    xy = swap(hop, to_schur)

    def held(on_near, on_far):
        return jnp.where(near, on_near, on_far)

    m = held(
        jnp.where(schur, hop, jnp.where(r < 2, q, xq)),
        jnp.where(schur, hop_far, zq),
    )
    m = after(jnp.where(corner, zq, m), hop_late)
    ym = swap(m, some(y_pair, lambda r, c: (r < 2 and c >= 4) or r == 0 or (r == 2 and c not in (2, 3))))
    n = jnp.concatenate([jnp.where(even, m[:1], ym[:1]), jnp.where(even, ym, m)], 0)
    late = chosen([((0, c), (2, c)) for c in (2, 3)])
    n = jnp.where((r == 2) & (c < 4) & jnp.logical_not(near), swap(n, late), n)
    n = after(n, hop_later)
    n_other = swap(n, core_pair)

    state, factors = ([], []), []
    factor, state = chain_call(
        functools.partial(chain_early, 0, width), 0, width, [pos, n, n_other], [SMEM, VMEM, VMEM], state
    )
    factors.append(factor)

    cross = swap(
        jnp.where(corner, ym, zq),
        lambda r, c: x_pair(r, c) if c >= 4 else y_pair(r, c) if r >= 2 else (r, c),
    )
    g_near = after(hop_later, factor)
    g = held(
        jnp.where(schur, g_near, jnp.where(r < 2, zq, near_z)),
        jnp.where(schur, hop_late, jnp.where(r < 2, q, xq)),
    )
    yg = swap(g, some(y_pair, lambda r, c: r >= 2 or c < 4))
    factor, state = chain_call(
        functools.partial(chain_early, 1, width), 1, width, [pos, after(n, g, xz), n_other], [SMEM, VMEM, VMEM], state
    )
    factors.append(factor)
    yg = after(yg, factor)
    g2, g3 = jnp.where(even, g, yg), jnp.where(even, yg, g)
    g2_other, g3_other = swap(g2, core_pair), swap(g3, core_pair)
    g2 = after(g2, xy, g3_other)
    factor, state = chain_call(
        functools.partial(chain_later, 2, width), 2, width, [pos, g2, g2_other], [SMEM, VMEM, VMEM], state
    )
    factors.append(factor)
    crossed = jnp.stack([xq, xy, xz, after(cross, factor)])
    other = swap(crossed, some(core_pair, lambda r, c: r >= 2 and c >= 4))
    factor, state = chain_call(
        functools.partial(chain_later, 3, width), 3, width, [pos, g3, g3_other], [SMEM, VMEM, VMEM], state
    )
    factors.append(factor)
    invs, rights = state
    wide = 3 * width * SNODES
    inputs = [pos, stiffness, blocks, hop_far, zq, cross, crossed, other]
    return pl.pallas_call(
        functools.partial(box_tile, width),
        out_shape=jax.ShapeDtypeStruct((rows, width), f32),
        in_specs=[SMEM] + [VMEM] * (len(inputs) - 1 + 3 * SNODES),
        out_specs=VMEM,
        scratch_shapes=[
            pltpu.VMEM((rows + width, wide), bf16),
            pltpu.VMEM((width, wide), bf16),
            pltpu.VMEM((SNODES, rows + width, width), f32),
        ],
        compiler_params=TILE_PARAMS,
        cost_estimate=COST,
        name="tile",
    )(*inputs, *invs, *rights, *factors)


def solution(mesh):
    box = (mesh.shape["row"], mesh.shape["col"]) == (4, 8)

    def on_device(stiffness):
        rows, width = stiffness.shape
        return box_mesh(stiffness) if box and rows == 2 * width else any_mesh(stiffness)

    return jax.shard_map(
        on_device, mesh=mesh, in_specs=(P("row", "col"),), out_specs=P("row", "col"), check_vma=False
    )
```

```python
import functools

import jax
import jax.numpy as jnp
from jax import lax
from jax.experimental import pallas as pl
from jax.experimental.pallas import tpu as pltpu
from jax.sharding import PartitionSpec as P

SNODES = 4
LANES = 128
SUB = 8
f32 = jnp.float32
bf16 = jnp.bfloat16
VMEM = pl.BlockSpec(memory_space=pltpu.VMEM)
SMEM = pl.BlockSpec(memory_space=pltpu.SMEM)
PARAMS = pltpu.CompilerParams(vmem_limit_bytes=16 * 2**20)
TILE_PARAMS = pltpu.CompilerParams(vmem_limit_bytes=36 * 2**20)
COST = pl.CostEstimate(flops=1000, bytes_accessed=1024, transcendentals=0)


def lane_copy(tile, lane):
    return jnp.broadcast_to(tile[:, lane : lane + 1], (SUB, LANES))


def row_copy(tile, row):
    return jnp.broadcast_to(tile[row : row + 1, :], (SUB, LANES))


def factor_half(block):
    lane = lax.broadcasted_iota(jnp.int32, (SUB, LANES), 1)
    sub = lax.broadcasted_iota(jnp.int32, (SUB, LANES), 0)
    n = LANES // SUB
    tiles = [block[SUB * t : SUB * t + SUB, :] for t in range(n)]
    upper, inverse = [], []
    diag = [lane_copy(tiles[0], k) for k in range(SUB)]
    for p in range(n):
        rows, base = tiles[p], SUB * p
        up = jnp.zeros((SUB, LANES), f32)
        inv = up
        pivot_rows, scales, roots = [], [], []
        for j in range(SUB):
            at = base + j
            root = lax.rsqrt(row_copy(diag[j], j))
            column = diag[j] * root
            up_row = row_copy(rows, j) * root
            inv_row = jnp.where(lane == at, root, up_row)
            rows = jnp.where(lane == at, 0.0, rows) - column * inv_row
            scale = [None] * SUB
            for k in range(j + 1, SUB):
                scale[k] = row_copy(column, k)
                diag[k] = diag[k] - column * scale[k]
            up = jnp.where(sub == j, up_row, up)
            inv = jnp.where(sub == j, inv_row, inv)
            pivot_rows.append(jnp.where((lane > at) & (lane < base + SUB), 0.0, inv_row))
            scales.append(scale)
            roots.append(root)
        upper.append(up)
        inverse.append(inv)
        ahead = None
        for t in range(p + 1, n):
            left = [lane_copy(tiles[t], base + k) for k in range(SUB)]
            if t == p + 1:
                ahead = [lane_copy(tiles[t], base + SUB + k) for k in range(SUB)]
            rest = jnp.where((lane >= base) & (lane < base + SUB), 0.0, tiles[t])
            for j in range(SUB):
                column = left[j] * roots[j]
                rest = rest - column * pivot_rows[j]
                for k in range(j + 1, SUB):
                    left[k] = left[k] - column * scales[j][k]
                if t == p + 1:
                    for k in range(SUB):
                        ahead[k] = ahead[k] - column * row_copy(column, k)
            tiles[t] = rest
        diag = ahead
    return jnp.concatenate(upper, 0), jnp.concatenate(inverse, 0)


def split(x):
    high = x.astype(bf16)
    return high, (x - high.astype(f32)).astype(bf16)


def as_left(x):
    high, low = split(x)
    return jnp.concatenate([high, high, low], axis=1)


def as_right(x):
    high, low = split(x)
    return jnp.concatenate([high, low, high], axis=1)


def dot_t(left, right):
    return lax.dot_general(left, right, (((1,), (1,)), ((), ())), preferred_element_type=f32)


def dot_plain(a, b):
    def dot(x, y):
        return lax.dot_general(x, y, (((1,), (0,)), ((), ())), preferred_element_type=f32)

    (ah, al), (bh, bl) = split(a), split(b)
    return dot(ah, bh) + dot(ah, bl) + dot(al, bh)


def lower(x):
    row = lax.broadcasted_iota(jnp.int32, x.shape, 0)
    col = lax.broadcasted_iota(jnp.int32, x.shape, 1)
    return jnp.where(row >= col, x, 0.0)


def factor_block(block, factor_ref, col):
    h = LANES
    up_a, inv_a = factor_half(block[:h, :h])
    inv_a = lower(inv_a)
    low = dot_t(as_left(block[h:, :h]), as_right(inv_a))
    up_b, inv_b = factor_half(block[h:, h:] - dot_t(as_left(low), as_right(low)))
    inv_b = lower(inv_b)
    inv_low = -dot_plain(inv_b, dot_plain(low, inv_a))
    zero = jnp.zeros((h, h), f32)
    factor_ref[:h, col : col + h] = lower(up_a.T)
    factor_ref[:h, col + h : col + 2 * h] = zero
    factor_ref[h:, col : col + h] = low
    factor_ref[h:, col + h : col + 2 * h] = lower(up_b.T)
    return jnp.concatenate([jnp.concatenate([inv_a, zero], 1), jnp.concatenate([inv_low, inv_b], 1)], 0)


def chain_body(take, k, width, refs):
    inv_refs, right_refs = refs[:k], refs[k : 2 * k]
    factor_ref, inv_ref, right_ref, left = refs[2 * k :]
    w = width
    for j in range(k):
        rest = take(j)
        if j > 0:
            rest = rest - dot_t(left[:, : 3 * w * j], right_refs[j][:, : 3 * w * j])
        row = dot_t(as_left(rest), inv_refs[j][...])
        factor_ref[:, w * j : w * j + w] = row
        left[:, 3 * w * j : 3 * w * (j + 1)] = as_left(row)
        right_ref[:, 3 * w * j : 3 * w * (j + 1)] = as_right(row)
    block = take(k)
    if k > 0:
        block = block - dot_t(left[:, : 3 * w * k], right_ref[:, : 3 * w * k])
    else:
        right_ref[...] = jnp.zeros_like(right_ref)
    inv_ref[...] = as_right(factor_block(block, factor_ref, w * k))


def chain_call(kernel, k, width, inputs, specs, state):
    invs, rights = state
    wide = 3 * width * max(1, k)
    factor, inv, right = pl.pallas_call(
        kernel,
        out_shape=[
            jax.ShapeDtypeStruct((width, (k + 1) * width), f32),
            jax.ShapeDtypeStruct((width, 3 * width), bf16),
            jax.ShapeDtypeStruct((width, wide), bf16),
        ],
        in_specs=specs + [VMEM] * (2 * k),
        out_specs=[VMEM] * 3,
        scratch_shapes=[pltpu.VMEM((width, wide), bf16)],
        compiler_params=PARAMS,
        cost_estimate=COST,
        name=f"chain{k}",
    )(*inputs, *invs, *rights)
    return factor, (invs + [inv], rights + [right])


def solve_rows(take, rows, last, inv_refs, right_refs, left, right, factor_rows, width):
    w = width

    def step(k):
        rest = take(k)
        if k > 0:
            rest = rest - dot_t(left[:, : 3 * w * k], right_refs[k][:, : 3 * w * k])
        row = dot_t(as_left(rest), inv_refs[k][...])
        left[:, 3 * w * k : 3 * w * (k + 1)] = as_left(row)
        right[:, 3 * w * k : 3 * w * (k + 1)] = as_right(row[rows:])
        factor_rows(k, row[:rows])

    for k in range(SNODES):
        pl.when(last >= k)(functools.partial(step, k))


def write_tile(pos_ref, take, tile_ref, inv_refs, right_refs, factor_refs, out_ref, left, right, width):
    row_index, col_index = pos_ref[0], pos_ref[1]
    rows = out_ref.shape[0]
    blocks = rows // width
    inside = SNODES * width // rows
    top = row_index < inside

    @pl.when(jnp.logical_not(top))
    def _():
        def factor_rows(k, value):
            @pl.when(col_index == k)
            def _():
                out_ref[...] = value

        solve_rows(take, rows, col_index, inv_refs, right_refs, left, right, factor_rows, width)

        @pl.when(col_index >= SNODES)
        def _():
            out_ref[...] = tile_ref[...] - dot_t(left[:rows], right[...])

    @pl.when(top)
    def _():
        out_ref[...] = jnp.zeros_like(out_ref)
        for i in range(SNODES):
            for j in range(i + 1):

                @pl.when((row_index == i // blocks) & (col_index == j))
                def _():
                    at = (i % blocks) * width
                    out_ref[at : at + width, :] = factor_refs[i][:, j * width : (j + 1) * width]


def plain_chain(k, width, *refs):
    block_ref = refs[0]
    chain_body(lambda j: block_ref[:, j * width : (j + 1) * width], k, width, refs[1:])


def plain_tile(width, *refs):
    pos_ref, below_ref, tile_ref = refs[:3]
    n = SNODES
    inv_refs, right_refs, factor_refs = refs[3 : 3 + n], refs[3 + n : 3 + 2 * n], refs[3 + 2 * n : 3 + 3 * n]
    out_ref, left, right = refs[3 + 3 * n :]
    write_tile(
        pos_ref,
        lambda k: below_ref[:, k * width : (k + 1) * width],
        tile_ref, inv_refs, right_refs, factor_refs, out_ref, left, right, width,
    )


def tile_call(kernel, inputs, state, factors, rows, width):
    invs, rights = state
    wide = 3 * width * SNODES
    return pl.pallas_call(
        kernel,
        out_shape=jax.ShapeDtypeStruct((rows, width), f32),
        in_specs=[SMEM] + [VMEM] * (len(inputs) - 1 + 3 * SNODES),
        out_specs=VMEM,
        scratch_shapes=[pltpu.VMEM((rows + width, wide), bf16), pltpu.VMEM((width, wide), bf16)],
        compiler_params=TILE_PARAMS,
        cost_estimate=COST,
        name="tile",
    )(*inputs, *invs, *rights, *factors)


def any_mesh(stiffness):
    rows, width = stiffness.shape
    row_index, col_index = lax.axis_index("row"), lax.axis_index("col")
    inside = SNODES * width // rows
    zero = jnp.zeros_like(stiffness)
    own_rows = lax.psum(
        jnp.concatenate([jnp.where(col_index == j, stiffness, zero) for j in range(SNODES)], 1), "col"
    )
    window = lax.psum(
        jnp.concatenate([jnp.where(row_index == i, own_rows, jnp.zeros_like(own_rows)) for i in range(inside)], 0), "row"
    )
    own_cols = lax.psum(jnp.concatenate([jnp.where(row_index == i, stiffness, zero) for i in range(inside)], 0), "row")
    state, factors = ([], []), []
    for k in range(SNODES):
        block = window[k * width : (k + 1) * width, : (k + 1) * width]
        factor, state = chain_call(functools.partial(plain_chain, k, width), k, width, [block], [VMEM], state)
        factors.append(factor)
    below = jnp.concatenate([own_rows, own_cols.T], 0)
    pos = jnp.stack([row_index, col_index]).astype(jnp.int32)
    return tile_call(
        functools.partial(plain_tile, width), [pos, below, stiffness], state, factors, rows, width
    )


def chain_early(k, width, pos_ref, a_ref, b_ref, *refs):
    even = (pos_ref[0] % 2) == 0
    chain_body(lambda j: jnp.where(even, a_ref[k + j], b_ref[k + j]), k, width, refs)


def chain_later(k, width, pos_ref, a_ref, b_ref, *refs):
    core = pos_ref[0] % 2
    chain_body(lambda j: jnp.where(core == j // 2, a_ref[j % 2], b_ref[j % 2]), k, width, refs)


def box_tile(width, *refs):
    pos_ref, tile_ref = refs[:2]
    below, crossed, other = refs[2:6], refs[6], refs[7]
    rest = refs[8:]
    n = SNODES
    inv_refs, right_refs, factor_refs = rest[:n], rest[n : 2 * n], rest[2 * n : 3 * n]
    out_ref, left, right, work = rest[3 * n :]
    row_index, col_index = pos_ref[0], pos_ref[1]
    core = row_index % 2
    w = width

    @pl.when((row_index >= 2) & (col_index < n))
    def _():
        for m in range(4):
            k = col_index ^ m
            work[k, :w, :] = below[m][0]
            work[k, w : 2 * w, :] = below[m][1]

    @pl.when((row_index >= 2) & (col_index >= n))
    def _():
        for m in range(4):
            column = (col_index ^ m) - n

            def place(at):
                for k in range(n):
                    work[k, at * w : (at + 1) * w, :] = jnp.where(core == k // 2, crossed[m, k % 2], other[m, k % 2])

            if m == 0:
                place(2)
            for at in range(2):
                pl.when(column == 2 * core + at)(functools.partial(place, at))

    write_tile(
        pos_ref, lambda k: work[k], tile_ref, inv_refs, right_refs, factor_refs, out_ref, left, right, width
    )


def swap(x, pair):
    perm = []
    for r in range(4):
        for c in range(8):
            pr, pc = pair(r, c)
            if (pr, pc) != (r, c):
                perm.append((r * 8 + c, pr * 8 + pc))
    return lax.ppermute(x, ("row", "col"), perm)


def core_pair(r, c):
    return r ^ 1, c


def x_pair(r, c):
    return r ^ 2, c


def y_pair(r, c):
    return r, c ^ 1


def z_pair(r, c):
    return r, c ^ 2


def after(x, *others):
    return lax.optimization_barrier((x, *others))[0]


def some(pair, members):
    return lambda r, c: pair(r, c) if members(r, c) else (r, c)


def chosen(pairs):
    table = {a: b for p, q in pairs for a, b in ((p, q), (q, p))}
    return lambda r, c: table.get((r, c), (r, c))


def box_mesh(stiffness):
    rows, width = stiffness.shape
    r, c = lax.axis_index("row"), lax.axis_index("col")
    pos = jnp.stack([r, c]).astype(jnp.int32)
    blocks = stiffness.reshape(2, width, width)
    even, near = c % 2 == 0, (c // 2) % 2 == 0
    schur, corner = (r >= 2) & (c >= 4), (r < 2) & (c >= 4)
    q = jnp.where(r < 2, blocks.transpose(0, 2, 1), blocks)

    below = [((r, c), (r, c + 1)) for r in (2, 3) for c in (0, 2)]
    hop = swap(q, chosen([((0, 0), (2, 4)), ((0, 1), (2, 5))]))
    hop_far = swap(q, chosen([((0, 0), (2, 6)), ((0, 1), (2, 7))] + below))
    zq = swap(q, lambda r, c: z_pair(r, c) if (r < 2 or c < 4) and not (r == 1 and c < 2) else (r, c))
    xq = swap(q, x_pair)
    hop_late = swap(xq, chosen([((r, c), (r, c + 4)) for r in (2, 3) for c in (2, 3)]))
    hop_later = swap(xq, chosen([((r, c), (r, c + 2)) for r in (2, 3) for c in (2, 3)]))
    to_schur = some(x_pair, lambda r, c: c >= 4)
    near_z = swap(zq, some(x_pair, lambda r, c: c < 2))
    xz = swap(zq, to_schur)
    xy = swap(xq, some(y_pair, lambda r, c: r >= 2 and c >= 4))

    def held(on_near, on_far):
        return jnp.where(near, on_near, on_far)

    m = held(
        jnp.where(schur, hop, jnp.where(r < 2, q, xq)),
        jnp.where(schur, hop_far, zq),
    )
    m = after(jnp.where(corner, zq, m), hop_late)
    ym = swap(m, some(y_pair, lambda r, c: (r < 2 and c >= 4) or r == 0 or (r == 2 and c not in (2, 3))))
    n = jnp.concatenate([jnp.where(even, m[:1], ym[:1]), jnp.where(even, ym, m)], 0)
    late = chosen([((0, c), (2, c)) for c in (2, 3)])
    n = jnp.where((r == 2) & (c < 4) & jnp.logical_not(near), swap(n, late), n)
    n = after(n, hop_later)
    n_other = swap(n, core_pair)

    state, factors = ([], []), []
    factor, state = chain_call(
        functools.partial(chain_early, 0, width), 0, width, [pos, n, n_other], [SMEM, VMEM, VMEM], state
    )
    factors.append(factor)

    cross = swap(
        jnp.where(corner, ym, zq),
        lambda r, c: x_pair(r, c) if c >= 4 else y_pair(r, c) if r >= 2 else (r, c),
    )
    g_near = after(hop_later, factor)
    g = held(
        jnp.where(schur, g_near, jnp.where(r < 2, zq, near_z)),
        jnp.where(schur, hop_late, jnp.where(r < 2, q, xq)),
    )
    yg = swap(g, some(y_pair, lambda r, c: r >= 2 or c < 4))
    factor, state = chain_call(
        functools.partial(chain_early, 1, width), 1, width, [pos, after(n, g, xz, xy), n_other], [SMEM, VMEM, VMEM], state
    )
    factors.append(factor)
    yg = after(yg, factor)
    g2, g3 = jnp.where(even, g, yg), jnp.where(even, yg, g)
    g2_other, g3_other = swap(g2, core_pair), swap(g3, core_pair)
    g2 = after(g2, cross, g3_other)
    factor, state = chain_call(
        functools.partial(chain_later, 2, width), 2, width, [pos, g2, g2_other], [SMEM, VMEM, VMEM], state
    )
    factors.append(factor)
    crossed = jnp.stack([xq, xy, xz, after(cross, factor)])
    other = swap(crossed, some(core_pair, lambda r, c: r >= 2 and c >= 4))
    factor, state = chain_call(
        functools.partial(chain_later, 3, width), 3, width, [pos, g3, g3_other], [SMEM, VMEM, VMEM], state
    )
    factors.append(factor)
    invs, rights = state
    wide = 3 * width * SNODES
    inputs = [pos, stiffness, blocks, hop_far, zq, cross, crossed, other]
    return pl.pallas_call(
        functools.partial(box_tile, width),
        out_shape=jax.ShapeDtypeStruct((rows, width), f32),
        in_specs=[SMEM] + [VMEM] * (len(inputs) - 1 + 3 * SNODES),
        out_specs=VMEM,
        scratch_shapes=[
            pltpu.VMEM((rows + width, wide), bf16),
            pltpu.VMEM((width, wide), bf16),
            pltpu.VMEM((SNODES, rows + width, width), f32),
        ],
        compiler_params=TILE_PARAMS,
        cost_estimate=COST,
        name="tile",
    )(*inputs, *invs, *rights, *factors)


def solution(mesh):
    box = (mesh.shape["row"], mesh.shape["col"]) == (4, 8)

    def on_device(stiffness):
        rows, width = stiffness.shape
        return box_mesh(stiffness) if box and rows == 2 * width else any_mesh(stiffness)

    return jax.shard_map(
        on_device, mesh=mesh, in_specs=(P("row", "col"),), out_specs=P("row", "col"), check_vma=False
    )
```

```python
import functools

import jax
import jax.numpy as jnp
from jax import lax
from jax.experimental import pallas as pl
from jax.experimental.pallas import tpu as pltpu
from jax.sharding import PartitionSpec as P

SNODES = 4
LANES = 128
SUB = 8
f32 = jnp.float32
bf16 = jnp.bfloat16
VMEM = pl.BlockSpec(memory_space=pltpu.VMEM)
SMEM = pl.BlockSpec(memory_space=pltpu.SMEM)
PARAMS = pltpu.CompilerParams(vmem_limit_bytes=16 * 2**20)
TILE_PARAMS = pltpu.CompilerParams(vmem_limit_bytes=36 * 2**20)
COST = pl.CostEstimate(flops=1000, bytes_accessed=1024, transcendentals=0)


def lane_copy(tile, lane):
    return jnp.broadcast_to(tile[:, lane : lane + 1], (SUB, LANES))


def row_copy(tile, row):
    return jnp.broadcast_to(tile[row : row + 1, :], (SUB, LANES))


def factor_half(block):
    lane = lax.broadcasted_iota(jnp.int32, (SUB, LANES), 1)
    sub = lax.broadcasted_iota(jnp.int32, (SUB, LANES), 0)
    n = LANES // SUB
    tiles = [block[SUB * t : SUB * t + SUB, :] for t in range(n)]
    upper, inverse = [], []
    diag = [lane_copy(tiles[0], k) for k in range(SUB)]
    for p in range(n):
        rows, base = tiles[p], SUB * p
        up = jnp.zeros((SUB, LANES), f32)
        inv = up
        pivot_rows, scales, roots = [], [], []
        for j in range(SUB):
            at = base + j
            root = lax.rsqrt(row_copy(diag[j], j))
            column = diag[j] * root
            up_row = row_copy(rows, j) * root
            inv_row = jnp.where(lane == at, root, up_row)
            rows = jnp.where(lane == at, 0.0, rows) - column * inv_row
            scale = [None] * SUB
            for k in range(j + 1, SUB):
                scale[k] = row_copy(column, k)
                diag[k] = diag[k] - column * scale[k]
            up = jnp.where(sub == j, up_row, up)
            inv = jnp.where(sub == j, inv_row, inv)
            pivot_rows.append(jnp.where((lane > at) & (lane < base + SUB), 0.0, inv_row))
            scales.append(scale)
            roots.append(root)
        upper.append(up)
        inverse.append(inv)
        ahead = None
        for t in range(p + 1, n):
            left = [lane_copy(tiles[t], base + k) for k in range(SUB)]
            if t == p + 1:
                ahead = [lane_copy(tiles[t], base + SUB + k) for k in range(SUB)]
            rest = jnp.where((lane >= base) & (lane < base + SUB), 0.0, tiles[t])
            for j in range(SUB):
                column = left[j] * roots[j]
                rest = rest - column * pivot_rows[j]
                for k in range(j + 1, SUB):
                    left[k] = left[k] - column * scales[j][k]
                if t == p + 1:
                    for k in range(SUB):
                        ahead[k] = ahead[k] - column * row_copy(column, k)
            tiles[t] = rest
        diag = ahead
    return jnp.concatenate(upper, 0), jnp.concatenate(inverse, 0)


def split(x):
    high = x.astype(bf16)
    return high, (x - high.astype(f32)).astype(bf16)


def as_left(x):
    high, low = split(x)
    return jnp.concatenate([high, high, low], axis=1)


def as_right(x):
    high, low = split(x)
    return jnp.concatenate([high, low, high], axis=1)


def dot_t(left, right):
    return lax.dot_general(left, right, (((1,), (1,)), ((), ())), preferred_element_type=f32)


def dot_plain(a, b):
    def dot(x, y):
        return lax.dot_general(x, y, (((1,), (0,)), ((), ())), preferred_element_type=f32)

    (ah, al), (bh, bl) = split(a), split(b)
    return dot(ah, bh) + dot(ah, bl) + dot(al, bh)


def lower(x):
    row = lax.broadcasted_iota(jnp.int32, x.shape, 0)
    col = lax.broadcasted_iota(jnp.int32, x.shape, 1)
    return jnp.where(row >= col, x, 0.0)


def factor_block(block, factor_ref, col):
    h = LANES
    up_a, inv_a = factor_half(block[:h, :h])
    inv_a = lower(inv_a)
    low = dot_t(as_left(block[h:, :h]), as_right(inv_a))
    up_b, inv_b = factor_half(block[h:, h:] - dot_t(as_left(low), as_right(low)))
    inv_b = lower(inv_b)
    inv_low = -dot_plain(inv_b, dot_plain(low, inv_a))
    zero = jnp.zeros((h, h), f32)
    factor_ref[:h, col : col + h] = lower(up_a.T)
    factor_ref[:h, col + h : col + 2 * h] = zero
    factor_ref[h:, col : col + h] = low
    factor_ref[h:, col + h : col + 2 * h] = lower(up_b.T)
    return jnp.concatenate([jnp.concatenate([inv_a, zero], 1), jnp.concatenate([inv_low, inv_b], 1)], 0)


def chain_body(take, k, width, refs):
    inv_refs, right_refs = refs[:k], refs[k : 2 * k]
    factor_ref, inv_ref, right_ref, left = refs[2 * k :]
    w = width
    for j in range(k):
        rest = take(j)
        if j > 0:
            rest = rest - dot_t(left[:, : 3 * w * j], right_refs[j][:, : 3 * w * j])
        row = dot_t(as_left(rest), inv_refs[j][...])
        factor_ref[:, w * j : w * j + w] = row
        left[:, 3 * w * j : 3 * w * (j + 1)] = as_left(row)
        right_ref[:, 3 * w * j : 3 * w * (j + 1)] = as_right(row)
    block = take(k)
    if k > 0:
        block = block - dot_t(left[:, : 3 * w * k], right_ref[:, : 3 * w * k])
    else:
        right_ref[...] = jnp.zeros_like(right_ref)
    inv_ref[...] = as_right(factor_block(block, factor_ref, w * k))


def chain_call(kernel, k, width, inputs, specs, state):
    invs, rights = state
    wide = 3 * width * max(1, k)
    factor, inv, right = pl.pallas_call(
        kernel,
        out_shape=[
            jax.ShapeDtypeStruct((width, (k + 1) * width), f32),
            jax.ShapeDtypeStruct((width, 3 * width), bf16),
            jax.ShapeDtypeStruct((width, wide), bf16),
        ],
        in_specs=specs + [VMEM] * (2 * k),
        out_specs=[VMEM] * 3,
        scratch_shapes=[pltpu.VMEM((width, wide), bf16)],
        compiler_params=PARAMS,
        cost_estimate=COST,
        name=f"chain{k}",
    )(*inputs, *invs, *rights)
    return factor, (invs + [inv], rights + [right])


def solve_rows(take, rows, last, inv_refs, right_refs, left, right, factor_rows, width):
    w = width

    def step(k):
        rest = take(k)
        if k > 0:
            rest = rest - dot_t(left[:, : 3 * w * k], right_refs[k][:, : 3 * w * k])
        row = dot_t(as_left(rest), inv_refs[k][...])
        left[:, 3 * w * k : 3 * w * (k + 1)] = as_left(row)
        right[:, 3 * w * k : 3 * w * (k + 1)] = as_right(row[rows:])
        factor_rows(k, row[:rows])

    for k in range(SNODES):
        pl.when(last >= k)(functools.partial(step, k))


def write_tile(pos_ref, take, tile_ref, inv_refs, right_refs, factor_refs, out_ref, left, right, width):
    row_index, col_index = pos_ref[0], pos_ref[1]
    rows = out_ref.shape[0]
    blocks = rows // width
    inside = SNODES * width // rows
    top = row_index < inside

    @pl.when(jnp.logical_not(top))
    def _():
        def factor_rows(k, value):
            @pl.when(col_index == k)
            def _():
                out_ref[...] = value

        solve_rows(take, rows, col_index, inv_refs, right_refs, left, right, factor_rows, width)

        @pl.when(col_index >= SNODES)
        def _():
            out_ref[...] = tile_ref[...] - dot_t(left[:rows], right[...])

    @pl.when(top)
    def _():
        out_ref[...] = jnp.zeros_like(out_ref)
        for i in range(SNODES):
            for j in range(i + 1):

                @pl.when((row_index == i // blocks) & (col_index == j))
                def _():
                    at = (i % blocks) * width
                    out_ref[at : at + width, :] = factor_refs[i][:, j * width : (j + 1) * width]


def plain_chain(k, width, *refs):
    block_ref = refs[0]
    chain_body(lambda j: block_ref[:, j * width : (j + 1) * width], k, width, refs[1:])


def plain_tile(width, *refs):
    pos_ref, below_ref, tile_ref = refs[:3]
    n = SNODES
    inv_refs, right_refs, factor_refs = refs[3 : 3 + n], refs[3 + n : 3 + 2 * n], refs[3 + 2 * n : 3 + 3 * n]
    out_ref, left, right = refs[3 + 3 * n :]
    write_tile(
        pos_ref,
        lambda k: below_ref[:, k * width : (k + 1) * width],
        tile_ref, inv_refs, right_refs, factor_refs, out_ref, left, right, width,
    )


def tile_call(kernel, inputs, state, factors, rows, width):
    invs, rights = state
    wide = 3 * width * SNODES
    return pl.pallas_call(
        kernel,
        out_shape=jax.ShapeDtypeStruct((rows, width), f32),
        in_specs=[SMEM] + [VMEM] * (len(inputs) - 1 + 3 * SNODES),
        out_specs=VMEM,
        scratch_shapes=[pltpu.VMEM((rows + width, wide), bf16), pltpu.VMEM((width, wide), bf16)],
        compiler_params=TILE_PARAMS,
        cost_estimate=COST,
        name="tile",
    )(*inputs, *invs, *rights, *factors)


def any_mesh(stiffness):
    rows, width = stiffness.shape
    row_index, col_index = lax.axis_index("row"), lax.axis_index("col")
    inside = SNODES * width // rows
    zero = jnp.zeros_like(stiffness)
    own_rows = lax.psum(
        jnp.concatenate([jnp.where(col_index == j, stiffness, zero) for j in range(SNODES)], 1), "col"
    )
    window = lax.psum(
        jnp.concatenate([jnp.where(row_index == i, own_rows, jnp.zeros_like(own_rows)) for i in range(inside)], 0), "row"
    )
    own_cols = lax.psum(jnp.concatenate([jnp.where(row_index == i, stiffness, zero) for i in range(inside)], 0), "row")
    state, factors = ([], []), []
    for k in range(SNODES):
        block = window[k * width : (k + 1) * width, : (k + 1) * width]
        factor, state = chain_call(functools.partial(plain_chain, k, width), k, width, [block], [VMEM], state)
        factors.append(factor)
    below = jnp.concatenate([own_rows, own_cols.T], 0)
    pos = jnp.stack([row_index, col_index]).astype(jnp.int32)
    return tile_call(
        functools.partial(plain_tile, width), [pos, below, stiffness], state, factors, rows, width
    )


def chain_early(k, width, pos_ref, a_ref, b_ref, *refs):
    even = (pos_ref[0] % 2) == 0
    chain_body(lambda j: jnp.where(even, a_ref[k + j], b_ref[k + j]), k, width, refs)


def chain_later(k, width, pos_ref, a_ref, b_ref, *refs):
    core = pos_ref[0] % 2
    chain_body(lambda j: jnp.where(core == j // 2, a_ref[j % 2], b_ref[j % 2]), k, width, refs)


def box_tile(width, *refs):
    pos_ref, tile_ref = refs[:2]
    below, crossed, other = refs[2:6], refs[6], refs[7]
    rest = refs[8:]
    n = SNODES
    inv_refs, right_refs, factor_refs = rest[:n], rest[n : 2 * n], rest[2 * n : 3 * n]
    out_ref, left, right, work = rest[3 * n :]
    row_index, col_index = pos_ref[0], pos_ref[1]
    core = row_index % 2
    w = width

    @pl.when((row_index >= 2) & (col_index < n))
    def _():
        for m in range(4):
            k = col_index ^ m
            work[k, :w, :] = below[m][0]
            work[k, w : 2 * w, :] = below[m][1]

    @pl.when((row_index >= 2) & (col_index >= n))
    def _():
        for m in range(4):
            column = (col_index ^ m) - n

            def place(at):
                for k in range(n):
                    work[k, at * w : (at + 1) * w, :] = jnp.where(core == k // 2, crossed[m, k % 2], other[m, k % 2])

            if m == 0:
                place(2)
            for at in range(2):
                pl.when(column == 2 * core + at)(functools.partial(place, at))

    write_tile(
        pos_ref, lambda k: work[k], tile_ref, inv_refs, right_refs, factor_refs, out_ref, left, right, width
    )


def swap(x, pair):
    perm = []
    for r in range(4):
        for c in range(8):
            pr, pc = pair(r, c)
            if (pr, pc) != (r, c):
                perm.append((r * 8 + c, pr * 8 + pc))
    return lax.ppermute(x, ("row", "col"), perm)


def core_pair(r, c):
    return r ^ 1, c


def x_pair(r, c):
    return r ^ 2, c


def y_pair(r, c):
    return r, c ^ 1


def z_pair(r, c):
    return r, c ^ 2


def after(x, *others):
    return lax.optimization_barrier((x, *others))[0]


def some(pair, members):
    return lambda r, c: pair(r, c) if members(r, c) else (r, c)


def turn_blocks(pos_ref, block_ref, out_ref):
    top = pos_ref[0] < 2
    for b in range(2):
        out_ref[b] = jnp.where(top, block_ref[b].T, block_ref[b])


def chosen(pairs):
    table = {a: b for p, q in pairs for a, b in ((p, q), (q, p))}
    return lambda r, c: table.get((r, c), (r, c))


def box_mesh(stiffness):
    rows, width = stiffness.shape
    r, c = lax.axis_index("row"), lax.axis_index("col")
    pos = jnp.stack([r, c]).astype(jnp.int32)
    blocks = stiffness.reshape(2, width, width)
    even, near = c % 2 == 0, (c // 2) % 2 == 0
    schur, corner = (r >= 2) & (c >= 4), (r < 2) & (c >= 4)
    q = pl.pallas_call(
        turn_blocks,
        out_shape=jax.ShapeDtypeStruct(blocks.shape, f32),
        in_specs=[SMEM, VMEM],
        out_specs=VMEM,
        compiler_params=PARAMS,
        cost_estimate=COST,
        name="turn",
    )(pos, blocks)

    below = [((r, c), (r, c + 1)) for r in (2, 3) for c in (0, 2)]
    hop = swap(q, chosen([((0, 0), (2, 4)), ((0, 1), (2, 5))]))
    hop_far = swap(q, chosen([((0, 0), (2, 6)), ((0, 1), (2, 7))] + below))
    zq = swap(q, lambda r, c: z_pair(r, c) if (r < 2 or c < 4) and not (r == 1 and c < 2) else (r, c))
    xq = swap(q, x_pair)
    hop_late = swap(xq, chosen([((r, c), (r, c + 4)) for r in (2, 3) for c in (2, 3)]))
    hop_later = swap(xq, chosen([((r, c), (r, c + 2)) for r in (2, 3) for c in (2, 3)]))
    to_schur = some(x_pair, lambda r, c: c >= 4)
    near_z = swap(zq, some(x_pair, lambda r, c: c < 2))
    xz = swap(zq, to_schur)
    xy = swap(xq, some(y_pair, lambda r, c: r >= 2 and c >= 4))

    def held(on_near, on_far):
        return jnp.where(near, on_near, on_far)

    m = held(
        jnp.where(schur, hop, jnp.where(r < 2, q, xq)),
        jnp.where(schur, hop_far, zq),
    )
    m = after(jnp.where(corner, zq, m), hop_late)
    ym = swap(m, some(y_pair, lambda r, c: (r < 2 and c >= 4) or r == 0 or (r == 2 and c not in (2, 3))))
    n = jnp.concatenate([jnp.where(even, m[:1], ym[:1]), jnp.where(even, ym, m)], 0)
    late = chosen([((0, c), (2, c)) for c in (2, 3)])
    n = jnp.where((r == 2) & (c < 4) & jnp.logical_not(near), swap(n, late), n)
    n = after(n, hop_later)
    n_other = swap(n, core_pair)

    state, factors = ([], []), []
    factor, state = chain_call(
        functools.partial(chain_early, 0, width), 0, width, [pos, n, n_other], [SMEM, VMEM, VMEM], state
    )
    factors.append(factor)

    cross = swap(
        jnp.where(corner, ym, zq),
        lambda r, c: x_pair(r, c) if c >= 4 else y_pair(r, c) if r >= 2 else (r, c),
    )
    g_near = after(hop_later, factor)
    g = held(
        jnp.where(schur, g_near, jnp.where(r < 2, zq, near_z)),
        jnp.where(schur, hop_late, jnp.where(r < 2, q, xq)),
    )
    yg = swap(g, some(y_pair, lambda r, c: r >= 2 or c < 4))
    factor, state = chain_call(
        functools.partial(chain_early, 1, width), 1, width, [pos, after(n, g, xz, xy), n_other], [SMEM, VMEM, VMEM], state
    )
    factors.append(factor)
    yg = after(yg, factor)
    g2, g3 = jnp.where(even, g, yg), jnp.where(even, yg, g)
    g2_other, g3_other = swap(g2, core_pair), swap(g3, core_pair)
    g2 = after(g2, cross, g3_other)
    factor, state = chain_call(
        functools.partial(chain_later, 2, width), 2, width, [pos, g2, g2_other], [SMEM, VMEM, VMEM], state
    )
    factors.append(factor)
    crossed = jnp.stack([xq, xy, xz, after(cross, factor)])
    other = swap(crossed, some(core_pair, lambda r, c: r >= 2 and c >= 4))
    factor, state = chain_call(
        functools.partial(chain_later, 3, width), 3, width, [pos, g3, g3_other], [SMEM, VMEM, VMEM], state
    )
    factors.append(factor)
    invs, rights = state
    wide = 3 * width * SNODES
    inputs = [pos, stiffness, blocks, hop_far, zq, cross, crossed, other]
    return pl.pallas_call(
        functools.partial(box_tile, width),
        out_shape=jax.ShapeDtypeStruct((rows, width), f32),
        in_specs=[SMEM] + [VMEM] * (len(inputs) - 1 + 3 * SNODES),
        out_specs=VMEM,
        scratch_shapes=[
            pltpu.VMEM((rows + width, wide), bf16),
            pltpu.VMEM((width, wide), bf16),
            pltpu.VMEM((SNODES, rows + width, width), f32),
        ],
        compiler_params=TILE_PARAMS,
        cost_estimate=COST,
        name="tile",
    )(*inputs, *invs, *rights, *factors)


def solution(mesh):
    box = (mesh.shape["row"], mesh.shape["col"]) == (4, 8)

    def on_device(stiffness):
        rows, width = stiffness.shape
        return box_mesh(stiffness) if box and rows == 2 * width else any_mesh(stiffness)

    return jax.shard_map(
        on_device, mesh=mesh, in_specs=(P("row", "col"),), out_specs=P("row", "col"), check_vma=False
    )
```

```python
import functools

import jax
import jax.numpy as jnp
from jax import lax
from jax.experimental import pallas as pl
from jax.experimental.pallas import tpu as pltpu
from jax.sharding import PartitionSpec as P

SNODES = 4
LANES = 128
SUB = 8
f32 = jnp.float32
bf16 = jnp.bfloat16
VMEM = pl.BlockSpec(memory_space=pltpu.VMEM)
SMEM = pl.BlockSpec(memory_space=pltpu.SMEM)
PARAMS = pltpu.CompilerParams(vmem_limit_bytes=16 * 2**20)
TILE_PARAMS = pltpu.CompilerParams(vmem_limit_bytes=28 * 2**20)
COST = pl.CostEstimate(flops=1000, bytes_accessed=1024, transcendentals=0)


def lane_copy(tile, lane):
    return jnp.broadcast_to(tile[:, lane : lane + 1], (SUB, LANES))


def row_copy(tile, row):
    return jnp.broadcast_to(tile[row : row + 1, :], (SUB, LANES))


def factor_half(block):
    lane = lax.broadcasted_iota(jnp.int32, (SUB, LANES), 1)
    sub = lax.broadcasted_iota(jnp.int32, (SUB, LANES), 0)
    n = LANES // SUB
    tiles = [block[SUB * t : SUB * t + SUB, :] for t in range(n)]
    upper, inverse = [], []
    diag = [lane_copy(tiles[0], k) for k in range(SUB)]
    for p in range(n):
        rows, base = tiles[p], SUB * p
        up = jnp.zeros((SUB, LANES), f32)
        inv = up
        pivot_rows, scales, roots = [], [], []
        for j in range(SUB):
            at = base + j
            root = lax.rsqrt(row_copy(diag[j], j))
            column = diag[j] * root
            up_row = row_copy(rows, j) * root
            inv_row = jnp.where(lane == at, root, up_row)
            rows = jnp.where(lane == at, 0.0, rows) - column * inv_row
            scale = [None] * SUB
            for k in range(j + 1, SUB):
                scale[k] = row_copy(column, k)
                diag[k] = diag[k] - column * scale[k]
            up = jnp.where(sub == j, up_row, up)
            inv = jnp.where(sub == j, inv_row, inv)
            pivot_rows.append(jnp.where((lane > at) & (lane < base + SUB), 0.0, inv_row))
            scales.append(scale)
            roots.append(root)
        upper.append(up)
        inverse.append(inv)
        ahead = None
        for t in range(p + 1, n):
            left = [lane_copy(tiles[t], base + k) for k in range(SUB)]
            if t == p + 1:
                ahead = [lane_copy(tiles[t], base + SUB + k) for k in range(SUB)]
            rest = jnp.where((lane >= base) & (lane < base + SUB), 0.0, tiles[t])
            for j in range(SUB):
                column = left[j] * roots[j]
                rest = rest - column * pivot_rows[j]
                for k in range(j + 1, SUB):
                    left[k] = left[k] - column * scales[j][k]
                if t == p + 1:
                    for k in range(SUB):
                        ahead[k] = ahead[k] - column * row_copy(column, k)
            tiles[t] = rest
        diag = ahead
    return jnp.concatenate(upper, 0), jnp.concatenate(inverse, 0)


def split(x):
    high = x.astype(bf16)
    return high, (x - high.astype(f32)).astype(bf16)


def as_left(x):
    high, low = split(x)
    return jnp.concatenate([high, high, low], axis=1)


def as_right(x):
    high, low = split(x)
    return jnp.concatenate([high, low, high], axis=1)


def dot_t(left, right):
    return lax.dot_general(left, right, (((1,), (1,)), ((), ())), preferred_element_type=f32)


def dot_plain(a, b):
    def dot(x, y):
        return lax.dot_general(x, y, (((1,), (0,)), ((), ())), preferred_element_type=f32)

    (ah, al), (bh, bl) = split(a), split(b)
    return dot(ah, bh) + dot(ah, bl) + dot(al, bh)


def lower(x):
    row = lax.broadcasted_iota(jnp.int32, x.shape, 0)
    col = lax.broadcasted_iota(jnp.int32, x.shape, 1)
    return jnp.where(row >= col, x, 0.0)


def factor_block(block, factor_ref, col):
    h = LANES
    up_a, inv_a = factor_half(block[:h, :h])
    inv_a = lower(inv_a)
    low = dot_t(as_left(block[h:, :h]), as_right(inv_a))
    up_b, inv_b = factor_half(block[h:, h:] - dot_t(as_left(low), as_right(low)))
    inv_b = lower(inv_b)
    inv_low = -dot_plain(inv_b, dot_plain(low, inv_a))
    zero = jnp.zeros((h, h), f32)
    factor_ref[:h, col : col + h] = lower(up_a.T)
    factor_ref[:h, col + h : col + 2 * h] = zero
    factor_ref[h:, col : col + h] = low
    factor_ref[h:, col + h : col + 2 * h] = lower(up_b.T)
    return jnp.concatenate([jnp.concatenate([inv_a, zero], 1), jnp.concatenate([inv_low, inv_b], 1)], 0)


def chain_body(take, k, width, refs):
    inv_refs, right_refs = refs[:k], refs[k : 2 * k]
    factor_ref, inv_ref, right_ref, left = refs[2 * k :]
    w = width
    for j in range(k):
        rest = take(j)
        if j > 0:
            rest = rest - dot_t(left[:, : 3 * w * j], right_refs[j][:, : 3 * w * j])
        row = dot_t(as_left(rest), inv_refs[j][...])
        factor_ref[:, w * j : w * j + w] = row
        left[:, 3 * w * j : 3 * w * (j + 1)] = as_left(row)
        right_ref[:, 3 * w * j : 3 * w * (j + 1)] = as_right(row)
    block = take(k)
    if k > 0:
        block = block - dot_t(left[:, : 3 * w * k], right_ref[:, : 3 * w * k])
    else:
        right_ref[...] = jnp.zeros_like(right_ref)
    inv_ref[...] = as_right(factor_block(block, factor_ref, w * k))


def chain_call(kernel, k, width, inputs, specs, state):
    invs, rights = state
    wide = 3 * width * max(1, k)
    factor, inv, right = pl.pallas_call(
        kernel,
        out_shape=[
            jax.ShapeDtypeStruct((width, (k + 1) * width), f32),
            jax.ShapeDtypeStruct((width, 3 * width), bf16),
            jax.ShapeDtypeStruct((width, wide), bf16),
        ],
        in_specs=specs + [VMEM] * (2 * k),
        out_specs=[VMEM] * 3,
        scratch_shapes=[pltpu.VMEM((width, wide), bf16)],
        compiler_params=PARAMS,
        cost_estimate=COST,
        name=f"chain{k}",
    )(*inputs, *invs, *rights)
    return factor, (invs + [inv], rights + [right])


def solve_rows(take, rows, last, inv_refs, right_refs, left, right, factor_rows, width):
    w = width

    def step(k):
        rest = take(k)
        if k > 0:
            rest = rest - dot_t(left[:, : 3 * w * k], right_refs[k][:, : 3 * w * k])
        row = dot_t(as_left(rest), inv_refs[k][...])
        left[:, 3 * w * k : 3 * w * (k + 1)] = as_left(row)
        right[:, 3 * w * k : 3 * w * (k + 1)] = as_right(row[rows:])
        factor_rows(k, row[:rows])

    for k in range(SNODES):
        pl.when(last >= k)(functools.partial(step, k))


def write_tile(pos_ref, take, tile_ref, inv_refs, right_refs, factor_refs, out_ref, left, right, width):
    row_index, col_index = pos_ref[0], pos_ref[1]
    rows = out_ref.shape[0]
    blocks = rows // width
    inside = SNODES * width // rows
    top = row_index < inside

    @pl.when(jnp.logical_not(top))
    def _():
        def factor_rows(k, value):
            @pl.when(col_index == k)
            def _():
                out_ref[...] = value

        solve_rows(take, rows, col_index, inv_refs, right_refs, left, right, factor_rows, width)

        @pl.when(col_index >= SNODES)
        def _():
            out_ref[...] = tile_ref[...] - dot_t(left[:rows], right[...])

    @pl.when(top)
    def _():
        out_ref[...] = jnp.zeros_like(out_ref)
        for i in range(SNODES):
            for j in range(i + 1):

                @pl.when((row_index == i // blocks) & (col_index == j))
                def _():
                    at = (i % blocks) * width
                    out_ref[at : at + width, :] = factor_refs[i][:, j * width : (j + 1) * width]


def plain_chain(k, width, *refs):
    block_ref = refs[0]
    chain_body(lambda j: block_ref[:, j * width : (j + 1) * width], k, width, refs[1:])


def plain_tile(width, *refs):
    pos_ref, below_ref, tile_ref = refs[:3]
    n = SNODES
    inv_refs, right_refs, factor_refs = refs[3 : 3 + n], refs[3 + n : 3 + 2 * n], refs[3 + 2 * n : 3 + 3 * n]
    out_ref, left, right = refs[3 + 3 * n :]
    write_tile(
        pos_ref,
        lambda k: below_ref[:, k * width : (k + 1) * width],
        tile_ref, inv_refs, right_refs, factor_refs, out_ref, left, right, width,
    )


def tile_call(kernel, inputs, state, factors, rows, width):
    invs, rights = state
    wide = 3 * width * SNODES
    return pl.pallas_call(
        kernel,
        out_shape=jax.ShapeDtypeStruct((rows, width), f32),
        in_specs=[SMEM] + [VMEM] * (len(inputs) - 1 + 3 * SNODES),
        out_specs=VMEM,
        scratch_shapes=[pltpu.VMEM((rows + width, wide), bf16), pltpu.VMEM((width, wide), bf16)],
        compiler_params=TILE_PARAMS,
        cost_estimate=COST,
        name="tile",
    )(*inputs, *invs, *rights, *factors)


def any_mesh(stiffness):
    rows, width = stiffness.shape
    row_index, col_index = lax.axis_index("row"), lax.axis_index("col")
    inside = SNODES * width // rows
    zero = jnp.zeros_like(stiffness)
    own_rows = lax.psum(
        jnp.concatenate([jnp.where(col_index == j, stiffness, zero) for j in range(SNODES)], 1), "col"
    )
    window = lax.psum(
        jnp.concatenate([jnp.where(row_index == i, own_rows, jnp.zeros_like(own_rows)) for i in range(inside)], 0), "row"
    )
    own_cols = lax.psum(jnp.concatenate([jnp.where(row_index == i, stiffness, zero) for i in range(inside)], 0), "row")
    state, factors = ([], []), []
    for k in range(SNODES):
        block = window[k * width : (k + 1) * width, : (k + 1) * width]
        factor, state = chain_call(functools.partial(plain_chain, k, width), k, width, [block], [VMEM], state)
        factors.append(factor)
    below = jnp.concatenate([own_rows, own_cols.T], 0)
    pos = jnp.stack([row_index, col_index]).astype(jnp.int32)
    return tile_call(
        functools.partial(plain_tile, width), [pos, below, stiffness], state, factors, rows, width
    )


def chain_early(k, width, pos_ref, a_ref, b_ref, *refs):
    even = (pos_ref[0] % 2) == 0
    chain_body(lambda j: jnp.where(even, a_ref[k + j], b_ref[k + j]), k, width, refs)


def chain_later(k, width, pos_ref, a_ref, b_ref, *refs):
    core = pos_ref[0] % 2
    chain_body(lambda j: jnp.where(core == j // 2, a_ref[j % 2], b_ref[j % 2]), k, width, refs)


def box_tile(width, *refs):
    pos_ref, tile_ref = refs[:2]
    below, crossed, other = refs[2:6], refs[6], refs[7]
    rest = refs[8:]
    n = SNODES
    inv_refs, right_refs, factor_refs = rest[:n], rest[n : 2 * n], rest[2 * n : 3 * n]
    out_ref, left, right, work = rest[3 * n :]
    row_index, col_index = pos_ref[0], pos_ref[1]
    core = row_index % 2
    w = width

    @pl.when((row_index >= 2) & (col_index < n))
    def _():
        for m in range(4):
            k = col_index ^ m
            work[k, :w, :] = below[m][0]
            work[k, w : 2 * w, :] = below[m][1]

    @pl.when((row_index >= 2) & (col_index >= n))
    def _():
        for m in range(4):
            column = (col_index ^ m) - n

            def place(at):
                for k in range(n):
                    work[k, at * w : (at + 1) * w, :] = jnp.where(core == k // 2, crossed[m, k % 2], other[m, k % 2])

            if m == 0:
                place(2)
            for at in range(2):
                pl.when(column == 2 * core + at)(functools.partial(place, at))

    write_tile(
        pos_ref, lambda k: work[k], tile_ref, inv_refs, right_refs, factor_refs, out_ref, left, right, width
    )


def swap(x, pair):
    perm = []
    for r in range(4):
        for c in range(8):
            pr, pc = pair(r, c)
            if (pr, pc) != (r, c):
                perm.append((r * 8 + c, pr * 8 + pc))
    return lax.ppermute(x, ("row", "col"), perm)


def core_pair(r, c):
    return r ^ 1, c


def x_pair(r, c):
    return r ^ 2, c


def y_pair(r, c):
    return r, c ^ 1


def z_pair(r, c):
    return r, c ^ 2


def after(x, *others):
    return lax.optimization_barrier((x, *others))[0]


def some(pair, members):
    return lambda r, c: pair(r, c) if members(r, c) else (r, c)


def turn_blocks(pos_ref, block_ref, out_ref):
    top = pos_ref[0] < 2
    for b in range(2):
        out_ref[b] = jnp.where(top, block_ref[b].T, block_ref[b])


def chosen(pairs):
    table = {a: b for p, q in pairs for a, b in ((p, q), (q, p))}
    return lambda r, c: table.get((r, c), (r, c))


def box_mesh(stiffness):
    rows, width = stiffness.shape
    r, c = lax.axis_index("row"), lax.axis_index("col")
    pos = jnp.stack([r, c]).astype(jnp.int32)
    blocks = stiffness.reshape(2, width, width)
    even, near = c % 2 == 0, (c // 2) % 2 == 0
    schur, corner = (r >= 2) & (c >= 4), (r < 2) & (c >= 4)
    q = pl.pallas_call(
        turn_blocks,
        out_shape=jax.ShapeDtypeStruct(blocks.shape, f32),
        in_specs=[SMEM, VMEM],
        out_specs=VMEM,
        compiler_params=PARAMS,
        cost_estimate=COST,
        name="turn",
    )(pos, blocks)

    below = [((r, c), (r, c + 1)) for r in (2, 3) for c in (0, 2)]
    hop = swap(q, chosen([((0, 0), (2, 4)), ((0, 1), (2, 5))]))
    hop_far = swap(q, chosen([((0, 0), (2, 6)), ((0, 1), (2, 7))] + below))
    zq = swap(q, lambda r, c: z_pair(r, c) if (r < 2 or c < 4) and not (r == 1 and c < 2) else (r, c))
    xq = swap(q, x_pair)
    hop_late = swap(xq, chosen([((r, c), (r, c + 4)) for r in (2, 3) for c in (2, 3)]))
    hop_later = swap(xq, chosen([((r, c), (r, c + 2)) for r in (2, 3) for c in (2, 3)]))
    to_schur = some(x_pair, lambda r, c: c >= 4)
    near_z = swap(zq, some(x_pair, lambda r, c: c < 2))
    xz = swap(zq, to_schur)
    xy = swap(xq, some(y_pair, lambda r, c: r >= 2 and c >= 4))

    def held(on_near, on_far):
        return jnp.where(near, on_near, on_far)

    m = held(
        jnp.where(schur, hop, jnp.where(r < 2, q, xq)),
        jnp.where(schur, hop_far, zq),
    )
    m = after(jnp.where(corner, zq, m), hop_late)
    ym = swap(m, some(y_pair, lambda r, c: (r < 2 and c >= 4) or r == 0 or (r == 2 and c not in (2, 3))))
    n = jnp.concatenate([jnp.where(even, m[:1], ym[:1]), jnp.where(even, ym, m)], 0)
    late = chosen([((0, c), (2, c)) for c in (2, 3)])
    n = jnp.where((r == 2) & (c < 4) & jnp.logical_not(near), swap(n, late), n)
    n = after(n, hop_later)
    n_other = swap(n, core_pair)

    state, factors = ([], []), []
    factor, state = chain_call(
        functools.partial(chain_early, 0, width), 0, width, [pos, n, n_other], [SMEM, VMEM, VMEM], state
    )
    factors.append(factor)

    cross = swap(
        jnp.where(corner, ym, zq),
        lambda r, c: x_pair(r, c) if c >= 4 else y_pair(r, c) if r >= 2 else (r, c),
    )
    g_near = after(hop_later, factor)
    g = held(
        jnp.where(schur, g_near, jnp.where(r < 2, zq, near_z)),
        jnp.where(schur, hop_late, jnp.where(r < 2, q, xq)),
    )
    yg = swap(g, some(y_pair, lambda r, c: r >= 2 or c < 4))
    factor, state = chain_call(
        functools.partial(chain_early, 1, width), 1, width, [pos, after(n, g, xz, xy), n_other], [SMEM, VMEM, VMEM], state
    )
    factors.append(factor)
    yg = after(yg, factor)
    g2, g3 = jnp.where(even, g, yg), jnp.where(even, yg, g)
    g2_other, g3_other = swap(g2, core_pair), swap(g3, core_pair)
    g2 = after(g2, cross, g3_other)
    factor, state = chain_call(
        functools.partial(chain_later, 2, width), 2, width, [pos, g2, g2_other], [SMEM, VMEM, VMEM], state
    )
    factors.append(factor)
    crossed = jnp.stack([xq, xy, xz, after(cross, factor)])
    other = swap(crossed, some(core_pair, lambda r, c: r >= 2 and c >= 4))
    factor, state = chain_call(
        functools.partial(chain_later, 3, width), 3, width, [pos, g3, g3_other], [SMEM, VMEM, VMEM], state
    )
    factors.append(factor)
    invs, rights = state
    wide = 3 * width * SNODES
    inputs = [pos, stiffness, blocks, hop_far, zq, cross, crossed, other]
    return pl.pallas_call(
        functools.partial(box_tile, width),
        out_shape=jax.ShapeDtypeStruct((rows, width), f32),
        in_specs=[SMEM] + [VMEM] * (len(inputs) - 1 + 3 * SNODES),
        out_specs=VMEM,
        scratch_shapes=[
            pltpu.VMEM((rows + width, wide), bf16),
            pltpu.VMEM((width, wide), bf16),
            pltpu.VMEM((SNODES, rows + width, width), f32),
        ],
        compiler_params=TILE_PARAMS,
        cost_estimate=COST,
        name="tile",
    )(*inputs, *invs, *rights, *factors)


def solution(mesh):
    box = (mesh.shape["row"], mesh.shape["col"]) == (4, 8)

    def on_device(stiffness):
        rows, width = stiffness.shape
        return box_mesh(stiffness) if box and rows == 2 * width else any_mesh(stiffness)

    return jax.shard_map(
        on_device, mesh=mesh, in_specs=(P("row", "col"),), out_specs=P("row", "col"), check_vma=False
    )
```
